256 devices in a mesh: row: 16 (over x_lo, y, core), col: 16 (over z, x_hi).
Axes of the slice: x: 4 (x_hi: 2, x_lo: 2; x = x_hi * 2 + x_lo), y: 4, z: 8, core: 2. Of those that a mesh axis runs over, the one named last changes fastest.
Arguments:
- tokens: bfloat16 [4096, 5120], P('row', 'col'), may hold values from -6 to 6
- up_out: bfloat16 [4096, 13824], P('row', 'col'), may hold values from -6 to 6
- up_tangent: bfloat16 [4096, 13824], P('row', 'col'), may hold values from -6 to 6
- cotangent: bfloat16 [4096, 13824], P('row', 'col'), may hold values from -0.59765625 to 0.59765625
- cot_tangent: bfloat16 [4096, 13824], P('row', 'col'), may hold values from -0.59765625 to 0.59765625
- gate_weight: bfloat16 [5120, 13824], P('row', 'col'), may hold values from -0.078125 to 0.078125
- gate_direction: bfloat16 [5120, 13824], P('row', 'col'), may hold values from -0.078125 to 0.078125
Outputs:
- curvature: bfloat16 [5120, 13824], P('row', 'col')
- input_tangent: bfloat16 [4096, 5120], P('row', 'col')
The draws below stay inside these ranges and needn't reach their ends.
All inputs are finite; a program needn't handle non-finite values.
Results may differ from the reference program's by a relative error of at most 0.022.
Values may be sent and summed in bfloat16 or wider, within the bound.
No kernel may reach another device: no remote copies, remote signals or barrier semaphores. Data moves between devices by JAX's collectives and lax.ppermute only.
A program may use at most 128 MiB of HBM per device.

```python
import jax
import jax.numpy as jnp
from jax import lax

D = 5120
FF = 13824
TOK_DEV = 256
TOKENS = 4096
N_ROW = 16
N_COL = 16


def block_scale(key, dims, cuts, least, largest):
    def one(position, blocks):
        draws = jax.random.uniform(jax.random.fold_in(jax.random.fold_in(key, 6), position), (blocks,), jnp.float32, least / len(cuts), largest / len(cuts))
        return jnp.repeat(jnp.exp(draws), dims[position] // blocks).reshape((-1,) + (1,) * (len(dims) - position - 1))

    loudness = one(*cuts[0])
    for cut in cuts[1:]:
        loudness = loudness * one(*cut)
    return loudness


def noise(own_key, dims, scale, most, split=(), kind=jnp.bfloat16):
    result = scale * jax.random.normal(own_key, dims, jnp.float32)
    if split:
        result = result * block_scale(own_key, dims, split, -0.22, 0.18)
    return jnp.clip(result, -most, most).astype(kind)


def setup_inputs(seed: int = 0) -> dict:
    seeds = jax.random.split(jax.random.key(seed), 8)
    return {
        "tokens": noise(seeds[0], (TOKENS, D), 1.0, 6.0, ((0, 16), (1, 16))),
        "up_out": noise(seeds[1], (TOKENS, FF), 1.0, 6.0, ((0, 16), (1, 16))),
        "up_tangent": noise(seeds[2], (TOKENS, FF), 1.0, 6.0, ((0, 16), (1, 16))),
        "cotangent": noise(seeds[3], (TOKENS, FF), 0.1, 0.59765625, ((0, 16), (1, 16))),
        "cot_tangent": noise(seeds[4], (TOKENS, FF), 0.1, 0.59765625, ((0, 16), (1, 16))),
        "gate_weight": noise(seeds[5], (D, FF), D ** -0.5, 0.078125, ((0, 16), (1, 16))),
        "gate_direction": noise(seeds[6], (D, FF), D ** -0.5, 0.078125, ((0, 16), (1, 16))),
    }


def reference(tokens, up_out, up_tangent, cotangent, cot_tangent, gate_weight, gate_direction):
    gate = jnp.dot(tokens, gate_weight, preferred_element_type=jnp.float32)
    gate_dot = jnp.dot(tokens, gate_direction, preferred_element_type=jnp.float32)
    sig = jax.nn.sigmoid(gate)
    first = sig * (1.0 + gate * (1.0 - sig))
    second = sig * (1.0 - sig) * (2.0 + gate * (1.0 - 2.0 * sig))
    up_val = up_out.astype(jnp.float32)
    up_dir = up_tangent.astype(jnp.float32)
    cot_val = cotangent.astype(jnp.float32)
    cot_dir = cot_tangent.astype(jnp.float32)
    back = (cot_val * up_val * first).astype(jnp.bfloat16)
    back_dot = (cot_dir * up_val * first + cot_val * up_dir * first + cot_val * up_val * second * gate_dot).astype(jnp.bfloat16)

    def token_block(total, index):
        start = (index * TOK_DEV).astype(jnp.int32)
        rows = lax.dynamic_slice_in_dim(tokens, start, TOK_DEV, 0)
        grads = lax.dynamic_slice_in_dim(back_dot, start, TOK_DEV, 0)
        term = jnp.dot(rows.T, grads, preferred_element_type=jnp.float32).astype(jnp.bfloat16)
        term = lax.optimization_barrier(term)
        return total + term.astype(jnp.float32), None

    curv_sum, _ = lax.scan(token_block, jnp.zeros((D, FF), jnp.float32), jnp.arange(N_ROW, dtype=jnp.int32))
    curvature = curv_sum.astype(jnp.bfloat16)

    width = FF // N_COL

    def unit_block(total, index):
        start = (index * width).astype(jnp.int32)
        dirs = lax.dynamic_slice_in_dim(back_dot, start, width, 1)
        vals = lax.dynamic_slice_in_dim(back, start, width, 1)
        wpart = lax.dynamic_slice_in_dim(gate_weight, start, width, 1)
        vpart = lax.dynamic_slice_in_dim(gate_direction, start, width, 1)
        part = jnp.dot(dirs, wpart.T, preferred_element_type=jnp.float32) + jnp.dot(vals, vpart.T, preferred_element_type=jnp.float32)
        part = lax.optimization_barrier(part.astype(jnp.bfloat16))
        return total + part.astype(jnp.float32), None

    tan_sum, _ = lax.scan(unit_block, jnp.zeros((TOKENS, D), jnp.float32), jnp.arange(N_COL, dtype=jnp.int32))
    return curvature, tan_sum.astype(jnp.bfloat16)
```

```python
import jax
import jax.numpy as jnp
from jax import lax
from jax.sharding import Mesh, PartitionSpec as P

F32 = jnp.float32
SIZES = {"xl": 2, "y": 4, "c": 2, "z": 8, "xh": 2}
AXES = ("xl", "y", "c", "z", "xh")


def shift(x, axis, by):
    n = SIZES[axis]
    return lax.ppermute(x, axis, [(i, (i + by) % n) for i in range(n)])


def dot(left, right, dims):
    return lax.dot_general(left, right, (dims, ((), ())), preferred_element_type=F32)


def add_rows(total, part, start):
    rows = part.shape[0]
    pieces = [total[start:start + rows] + part.astype(F32)]
    if start:
        pieces.insert(0, total[:start])
    if start + rows < total.shape[0]:
        pieces.append(total[start + rows:])
    return jnp.concatenate(pieces, axis=0)


def on_device(tokens, up_out, up_tangent, cotangent, cot_tangent, gate_weight, gate_direction):
    xl, y, c, z, xh = (lax.axis_index(name) for name in AXES)
    depth, wide = gate_weight.shape
    mine = tokens.shape[0]
    half = depth // 2
    first_core = c == 0
    same = c == xh

    def gather_rows(own):
        up = shift(own, "y", -1)
        down = shift(own, "y", 1)
        over = shift(own, "xl", 1)
        far_low = shift(down[:half], "y", 1)
        far_high = shift(up[half:], "y", -1)
        over_up = shift(over, "y", -1)
        over_down = shift(over, "y", 1)
        far = jnp.concatenate([far_low, far_high], axis=0)
        over_far = shift(far, "xl", 1)
        return [own, up, far, down, over, over_up, over_far, over_down]

    weights = gather_rows(gate_weight)
    directions = gather_rows(gate_direction)

    turned = tokens.T
    swapped = shift(turned, "c", 1)
    pair = jnp.concatenate(
        [jnp.where(first_core, turned, swapped), jnp.where(first_core, swapped, turned)], axis=1
    )
    crossed = lax.ppermute(pair, ("c", "xh"), [(0, 1), (3, 2)])
    block = jnp.where(same, pair, crossed)
    ahead, behind = [block], [block]
    for _ in range(3):
        ahead.append(shift(ahead[-1], "z", -1))
        behind.append(shift(behind[-1], "z", 1))
    opposite = jnp.concatenate(
        [shift(behind[3][:half], "z", 1), shift(ahead[3][half:], "z", -1)], axis=0
    )
    token_blocks = jnp.stack(ahead + [opposite] + behind[:0:-1])

    def token_block(other, offset):
        place = jnp.bitwise_xor(xl, other) * 4 + (y + offset) % 4
        return lax.dynamic_index_in_dim(token_blocks, (place - z + 8) % 8, 0, keepdims=False)

    rows_of = [token_block(other, offset) for other in range(2) for offset in range(4)]
    early, late = (0, 1, 3, 4), (2, 5, 6, 7)

    def products(blocks):
        total = None
        for group in (early, late):
            left = jnp.concatenate([blocks[i] for i in group], axis=0)
            right = jnp.concatenate([rows_of[i] for i in group], axis=0)
            part = dot(left, right, ((0,), (0,)))
            total = part if total is None else total + part
        away = jnp.where(first_core, total[:, mine:], total[:, :mine])
        kept = jnp.where(first_core, total[:, :mine], total[:, mine:])
        return kept + shift(away, "c", 1)

    gate = products(weights)
    gate_dot = products(directions)

    sig = jax.nn.sigmoid(gate)
    first = sig * (1.0 + gate * (1.0 - sig))
    second = sig * (1.0 - sig) * (2.0 + gate * (1.0 - 2.0 * sig))
    up_val = up_out.T.astype(F32)
    up_dir = up_tangent.T.astype(F32)
    cot_val = cotangent.T.astype(F32)
    cot_dir = cot_tangent.T.astype(F32)
    back = (cot_val * up_val * first).astype(jnp.bfloat16)
    back_dot = (
        cot_dir * up_val * first + cot_val * up_dir * first + cot_val * up_val * second * gate_dot
    ).astype(jnp.bfloat16)

    def both_cores(x):
        other = shift(x, "c", 1)
        return jnp.concatenate(
            [jnp.where(first_core, x, other), jnp.where(first_core, other, x)], axis=1
        )

    back_dot = both_cores(back_dot)
    back = both_cores(back)

    low = jnp.bfloat16

    def curv(other, offset):
        return dot(rows_of[other * 4 + offset], back_dot, ((1,), (1,)))

    got_x = shift(curv(1, 2).astype(low), "xl", 1)
    got_down = shift(curv(1, 1).astype(low), "y", 1)
    got_up = shift(curv(1, 3).astype(low), "y", -1)
    far = (curv(0, 2) + got_x.astype(F32)).astype(low)
    far_down = shift(far[:half], "y", 1)
    far_up = shift(far[half:], "y", -1)
    over = (curv(1, 0) + got_down.astype(F32) + got_up.astype(F32)).astype(low)
    last_x = shift(over, "xl", 1)
    last_down = shift(add_rows(curv(0, 1), far_down, 0).astype(low), "y", 1)
    last_up = shift(add_rows(curv(0, 3), far_up, half).astype(low), "y", -1)
    curvature = (
        curv(0, 0) + last_x.astype(F32) + last_down.astype(F32) + last_up.astype(F32)
    ).astype(low)

    weight_stack = jnp.stack(weights)
    direction_stack = jnp.stack(directions)

    def tangent(offset):
        place = (z + offset) % 8
        index = jnp.bitwise_xor(place // 4, xl) * 4 + (place % 4 - y + 4) % 4
        w = lax.dynamic_index_in_dim(weight_stack, index, 0, keepdims=False)
        v = lax.dynamic_index_in_dim(direction_stack, index, 0, keepdims=False)
        return dot(w, back_dot, ((1,), (0,))) + dot(v, back, ((1,), (0,)))

    opposite = tangent(4).astype(low)
    plus = shift(opposite[:half], "z", 1)
    minus = shift(opposite[half:], "z", -1)
    plus = shift(add_rows(tangent(3), plus, 0).astype(low), "z", 1)
    minus = shift(add_rows(tangent(5), minus, half).astype(low), "z", -1)
    for offset in (2, 1):
        plus = shift((tangent(offset) + plus.astype(F32)).astype(low), "z", 1)
        minus = shift((tangent(8 - offset) + minus.astype(F32)).astype(low), "z", -1)
    total = tangent(0) + plus.astype(F32) + minus.astype(F32)
    crossed = lax.ppermute(total.astype(low), ("c", "xh"), [(1, 0), (2, 3)])
    total = (total + crossed.astype(F32)).astype(low)
    kept = jnp.where(first_core, total[:, :mine], total[:, mine:])
    away = jnp.where(first_core, total[:, mine:], total[:, :mine])
    arrived = lax.ppermute(away, ("c", "xh"), [(0, 2), (3, 1)])
    input_tangent = jnp.where(same, kept, arrived).T
    return (curvature, input_tangent)


def solution(mesh):
    fine = Mesh(mesh.devices.reshape([SIZES[name] for name in AXES]), AXES)
    spec = P(("xl", "y", "c"), ("z", "xh"))
    return jax.shard_map(
        on_device, mesh=fine, in_specs=(spec,) * 7, out_specs=(spec, spec), check_vma=False
    )
```

```python
import jax
import jax.numpy as jnp
from jax import lax
from jax.sharding import Mesh, PartitionSpec as P

F32 = jnp.float32
LOW = jnp.bfloat16
SIZES = {"xl": 2, "y": 4, "c": 2, "z": 8, "xh": 2}
AXES = ("xl", "y", "c", "z", "xh")


def swap(x, axis):
    return lax.ppermute(x, axis, [(0, 1), (1, 0)])


def step(x, axis, by):
    n = SIZES[axis]
    moves = [(c, i, (i + (by if c == 0 else -by)) % n) for c in range(2) for i in range(n)]
    if axis == "y":
        return lax.ppermute(x, ("y", "c"), [(2 * i + c, 2 * j + c) for c, i, j in moves])
    return lax.ppermute(x, ("c", "z"), [(n * c + i, n * c + j) for c, i, j in moves])


def dot(left, right, dims):
    return lax.dot_general(left, right, (dims, ((), ())), preferred_element_type=F32)


def add_rows(total, part, start):
    rows = part.shape[0]
    pieces = [total[start:start + rows] + part.astype(F32)]
    if start:
        pieces.insert(0, total[:start])
    if start + rows < total.shape[0]:
        pieces.append(total[start + rows:])
    return jnp.concatenate(pieces, axis=0)


def on_device(tokens, up_out, up_tangent, cotangent, cot_tangent, gate_weight, gate_direction):
    xl, y, c, z, xh = (lax.axis_index(name) for name in AXES)
    depth, wide = gate_weight.shape
    mine = tokens.shape[0]
    half = depth // 2
    first_core = c == 0
    same = c == xh
    sign = 1 - 2 * c

    own = jnp.concatenate([gate_weight, gate_direction], axis=0)
    one = step(own, "y", 1)
    two = step(own, "y", -1)
    over = swap(own, "xl")

    turned = tokens.T
    near = lax.ppermute(turned, ("c", "xh"), [(2, 0), (1, 3), (0, 1), (3, 2)])
    cross = lax.ppermute(turned, ("c", "xh"), [(2, 1), (1, 2)])
    kept = jnp.where(same, turned, cross)
    block = jnp.concatenate(
        [jnp.where(xh == 0, kept, near), jnp.where(xh == 0, near, kept)], axis=1
    )
    chain_a, chain_b = [block], [block]
    for _ in range(3):
        chain_a.append(step(chain_a[-1], "z", 1))
        chain_b.append(step(chain_b[-1], "z", -1))
    opposite = jnp.concatenate(
        [step(chain_a[3][:half], "z", 1), step(chain_b[3][half:], "z", -1)], axis=0
    )
    token_blocks = jnp.stack(chain_b + [opposite] + chain_a[:0:-1])

    far = jnp.concatenate([step(one[:depth], "y", 1), step(two[depth:], "y", -1)], axis=0)
    over_one = step(over, "y", 1)
    over_two = step(over, "y", -1)
    over_far = swap(far, "xl")
    pairs = [own, two, far, one, over, over_two, over_far, over_one]
    weights = [p[:depth] for p in pairs]
    directions = [p[depth:] for p in pairs]

    def token_block(other, offset):
        place = jnp.bitwise_xor(xl, other) * 4 + (y + sign * offset + 4) % 4
        index = (sign * (place - z) + 16) % 8
        return lax.dynamic_index_in_dim(token_blocks, index, 0, keepdims=False)

    rows_of = [token_block(other, offset) for other in range(2) for offset in range(4)]
    groups = ((0, 1, 3, 4), (2, 5, 7), (6,))

    def products(blocks):
        total = None
        for group in groups:
            left = jnp.concatenate([blocks[i] for i in group], axis=0)
            right = jnp.concatenate([rows_of[i] for i in group], axis=0)
            part = dot(left, right, ((0,), (0,)))
            total = part if total is None else total + part
        away = jnp.where(first_core, total[:, mine:], total[:, :mine])
        kept = jnp.where(first_core, total[:, :mine], total[:, mine:])
        return kept + swap(away, "c")

    gate = products(weights)
    gate_dot = products(directions)

    sig = jax.nn.sigmoid(gate)
    first = sig * (1.0 + gate * (1.0 - sig))
    second = sig * (1.0 - sig) * (2.0 + gate * (1.0 - 2.0 * sig))
    up_val = up_out.T.astype(F32)
    up_dir = up_tangent.T.astype(F32)
    cot_val = cotangent.T.astype(F32)
    cot_dir = cot_tangent.T.astype(F32)
    back = (cot_val * up_val * first).astype(LOW)
    back_dot = (
        cot_dir * up_val * first + cot_val * up_dir * first + cot_val * up_val * second * gate_dot
    ).astype(LOW)

    def both_cores(x):
        other = swap(x, "c")
        return jnp.concatenate(
            [jnp.where(first_core, x, other), jnp.where(first_core, other, x)], axis=1
        )

    back_dot = both_cores(back_dot)
    back = both_cores(back)

    def curv(other, offset):
        return dot(rows_of[other * 4 + offset], back_dot, ((1,), (1,)))

    got_x = swap(curv(1, 2).astype(LOW), "xl")
    got_one = step(curv(1, 1).astype(LOW), "y", 1)
    got_two = step(curv(1, 3).astype(LOW), "y", -1)
    far_sum = (curv(0, 2) + got_x.astype(F32)).astype(LOW)
    far_one = step(far_sum[:half], "y", 1)
    far_two = step(far_sum[half:], "y", -1)
    over_sum = (curv(1, 0) + got_one.astype(F32) + got_two.astype(F32)).astype(LOW)
    last_x = swap(over_sum, "xl")
    last_one = step(add_rows(curv(0, 1), far_one, 0).astype(LOW), "y", 1)
    last_two = step(add_rows(curv(0, 3), far_two, half).astype(LOW), "y", -1)
    curvature = (
        curv(0, 0) + last_x.astype(F32) + last_one.astype(F32) + last_two.astype(F32)
    ).astype(LOW)

    weight_stack = jnp.stack(weights)
    direction_stack = jnp.stack(directions)

    def tangent(offset):
        place = (z + sign * offset + 8) % 8
        index = jnp.bitwise_xor(place // 4, xl) * 4 + (sign * (place % 4 - y) + 8) % 4
        w = lax.dynamic_index_in_dim(weight_stack, index, 0, keepdims=False)
        v = lax.dynamic_index_in_dim(direction_stack, index, 0, keepdims=False)
        return dot(w, back_dot, ((1,), (0,))) + dot(v, back, ((1,), (0,)))

    opposite = tangent(4).astype(LOW)
    chain_a = step(opposite[:half], "z", 1)
    chain_b = step(opposite[half:], "z", -1)
    chain_a = step(add_rows(tangent(3), chain_a, 0).astype(LOW), "z", 1)
    chain_b = step(add_rows(tangent(-3), chain_b, half).astype(LOW), "z", -1)
    for offset in (2, 1):
        chain_a = step((tangent(offset) + chain_a.astype(F32)).astype(LOW), "z", 1)
        chain_b = step((tangent(-offset) + chain_b.astype(F32)).astype(LOW), "z", -1)
    total = tangent(0) + chain_a.astype(F32) + chain_b.astype(F32)
    left, right = total[:, :mine], total[:, mine:]
    of_own = jnp.where(first_core, left, right)
    of_other = jnp.where(first_core, right, left)
    sent = jnp.where(same, of_other, of_own).astype(LOW)
    near = lax.ppermute(sent, ("c", "xh"), [(1, 0), (2, 3), (0, 2), (3, 1)])
    cross = lax.ppermute(of_other.astype(LOW), ("c", "xh"), [(1, 2), (2, 1)])
    rest = jnp.where(same, of_own, cross.astype(F32))
    input_tangent = (rest + near.astype(F32)).astype(LOW).T
    return (curvature, input_tangent)


def solution(mesh):
    fine = Mesh(mesh.devices.reshape([SIZES[name] for name in AXES]), AXES)
    spec = P(("xl", "y", "c"), ("z", "xh"))
    return jax.shard_map(
        on_device, mesh=fine, in_specs=(spec,) * 7, out_specs=(spec, spec), check_vma=False
    )
```

```python
import jax
import jax.numpy as jnp
from jax import lax
from jax.experimental import pallas as pl
from jax.experimental.pallas import tpu as pltpu
from jax.sharding import Mesh, PartitionSpec as P

F32 = jnp.float32
LOW = jnp.bfloat16
SIZES = {"xl": 2, "y": 4, "c": 2, "z": 8, "xh": 2}
AXES = ("xl", "y", "c", "z", "xh")


def swap(x, axis):
    return lax.ppermute(x, axis, [(0, 1), (1, 0)])


def step(x, axis, by):
    n = SIZES[axis]
    moves = [(c, i, (i + (by if c == 0 else -by)) % n) for c in range(2) for i in range(n)]
    if axis == "y":
        return lax.ppermute(x, ("y", "c"), [(2 * i + c, 2 * j + c) for c, i, j in moves])
    return lax.ppermute(x, ("c", "z"), [(n * c + i, n * c + j) for c, i, j in moves])


def after(arrays):
    return lax.optimization_barrier(arrays)


def dot(left, right, dims):
    return lax.dot_general(left, right, (dims, ((), ())), preferred_element_type=F32)


def chosen_products_kernel(order, right, *refs):
    blocks, out, held, sems = refs[:8], refs[8], refs[9], refs[10]
    count = out.shape[0]

    def fetch(i):
        for j, block in enumerate(blocks):
            @pl.when(order[i] == j)
            def _():
                pltpu.make_async_copy(block, held.at[i % 2], sems.at[i % 2]).start()

    fetch(0)

    def body(i, carry):
        @pl.when(i + 1 < count)
        def _():
            fetch(i + 1)

        pltpu.make_async_copy(blocks[0], held.at[i % 2], sems.at[i % 2]).wait()
        out[i] = jnp.dot(held[i % 2], right[...], preferred_element_type=F32).astype(LOW)
        return carry

    lax.fori_loop(0, count, body, 0)


def chosen_products(order, right, blocks):
    count, (rows, depth), columns = order.shape[0], blocks[0].shape, right.shape[1]
    return pl.pallas_call(
        chosen_products_kernel,
        out_shape=jax.ShapeDtypeStruct((count, rows, columns), LOW),
        in_specs=[pl.BlockSpec(memory_space=pltpu.SMEM), pl.BlockSpec(memory_space=pltpu.VMEM)]
        + [pl.BlockSpec(memory_space=pl.ANY)] * 8,
        out_specs=pl.BlockSpec(memory_space=pltpu.VMEM),
        scratch_shapes=[pltpu.VMEM((2, rows, depth), LOW), pltpu.SemaphoreType.DMA((2,))],
        compiler_params=pltpu.CompilerParams(vmem_limit_bytes=24 * 2**20),
        cost_estimate=pl.CostEstimate(
            flops=2 * count * rows * depth * columns,
            bytes_accessed=2 * count * rows * (depth + columns),
            transcendentals=0,
        ),
    )(order, right, *blocks)


def add_rows(total, part, start):
    rows = part.shape[0]
    pieces = [total[start:start + rows] + part.astype(F32)]
    if start:
        pieces.insert(0, total[:start])
    if start + rows < total.shape[0]:
        pieces.append(total[start + rows:])
    return jnp.concatenate(pieces, axis=0)


def on_device(tokens, up_out, up_tangent, cotangent, cot_tangent, gate_weight, gate_direction):
    xl, y, c, z, xh = (lax.axis_index(name) for name in AXES)
    depth, wide = gate_weight.shape
    mine = tokens.shape[0]
    half = depth // 2
    first_core = c == 0
    same = c == xh
    sign = 1 - 2 * c

    room = -(-wide // 128) * 128
    gap = ((0, 0), (0, room - wide))
    own = jnp.concatenate([jnp.pad(gate_weight, gap), jnp.pad(gate_direction, gap)], axis=1)

    turned = tokens.T
    near = lax.ppermute(turned, ("c", "xh"), [(2, 0), (1, 3), (0, 1), (3, 2)])
    cross = lax.ppermute(turned, ("c", "xh"), [(2, 1), (1, 2)])
    kept = jnp.where(same, turned, cross)
    block = jnp.concatenate(
        [jnp.where(xh == 0, kept, near), jnp.where(xh == 0, near, kept)], axis=1
    )
    one = step(own, "y", 1)
    two = step(own, "y", -1)
    over = swap(own, "xl")
    a1, b1 = step(block, "z", 1), step(block, "z", -1)
    a2, b2 = step(a1, "z", 1), step(b1, "z", -1)
    far_one = step(one[:half], "y", 1)
    far_two = step(two[half:], "y", -1)
    a3, b3 = step(a2, "z", 1), step(b2, "z", -1)
    far = jnp.concatenate([far_one, far_two], axis=0)
    over, far, a3, b3 = after((over, far, a3, b3))
    over_far = swap(far, "xl")
    over_one = step(over, "y", 1)
    over_two = step(over, "y", -1)
    a4, b4 = step(a3[:half], "z", 1), step(b3[half:], "z", -1)
    opposite = jnp.concatenate([a4, b4], axis=0)
    token_blocks = jnp.stack([block, b1, b2, b3, opposite, a3, a2, a1])
    weights = [own, two, far, one, over, over_two, over_far, over_one]

    def token_block(other, offset):
        place = jnp.bitwise_xor(xl, other) * 4 + (y + sign * offset + 4) % 4
        index = (sign * (place - z) + 16) % 8
        return lax.dynamic_index_in_dim(token_blocks, index, 0, keepdims=False)

    rows_of = [token_block(other, offset) for other in range(2) for offset in range(4)]
    total = None
    for i in (0, 1, 3, 4, 2, 5, 7, 6):
        part = dot(weights[i], rows_of[i], ((0,), (0,)))
        total = part if total is None else total + part
    away = jnp.where(first_core, total[:, mine:], total[:, :mine])
    kept = jnp.where(first_core, total[:, :mine], total[:, mine:])
    both = kept + swap(away, "c")
    gate, gate_dot = both[:wide], both[room:room + wide]

    sig = jax.nn.sigmoid(gate)
    first = sig * (1.0 + gate * (1.0 - sig))
    second = sig * (1.0 - sig) * (2.0 + gate * (1.0 - 2.0 * sig))
    up_val = up_out.T.astype(F32)
    up_dir = up_tangent.T.astype(F32)
    cot_val = cotangent.T.astype(F32)
    cot_dir = cot_tangent.T.astype(F32)
    back = (cot_val * up_val * first).astype(LOW)
    back_dot = (
        cot_dir * up_val * first + cot_val * up_dir * first + cot_val * up_val * second * gate_dot
    ).astype(LOW)

    zeros = jnp.zeros((room - wide, mine), LOW)
    mixed = jnp.concatenate([back_dot, zeros, back, zeros], axis=0)
    other = swap(mixed, "c")
    mixed = jnp.concatenate(
        [jnp.where(first_core, mixed, other), jnp.where(first_core, other, mixed)], axis=1
    )
    back_dot = mixed[:wide]

    def number(offset):
        place = (z + sign * offset + 8) % 8
        return jnp.bitwise_xor(place // 4, xl) * 4 + (sign * (place % 4 - y) + 8) % 4

    offsets = (3, -3, 2, -2, 1, -1, 0)
    opposite = chosen_products(jnp.stack([number(4)]), mixed, weights)[0]
    back_dot, opposite = after((back_dot, opposite))
    chain_a = step(opposite[:half], "z", 1)
    chain_b = step(opposite[half:], "z", -1)

    def curv(other, offset):
        return dot(rows_of[other * 4 + offset], back_dot, ((1,), (1,)))

    got_x = swap(curv(1, 2).astype(LOW), "xl")
    got_one = step(curv(1, 1).astype(LOW), "y", 1)
    got_two = step(curv(1, 3).astype(LOW), "y", -1)
    far_sum = (curv(0, 2) + got_x.astype(F32)).astype(LOW)
    far_one = step(far_sum[:half], "y", 1)
    far_two = step(far_sum[half:], "y", -1)
    over_sum = (curv(1, 0) + got_one.astype(F32) + got_two.astype(F32)).astype(LOW)
    last_x = swap(over_sum, "xl")
    last_one = step(add_rows(curv(0, 1), far_one, 0).astype(LOW), "y", 1)
    last_two = step(add_rows(curv(0, 3), far_two, half).astype(LOW), "y", -1)
    curvature = (
        curv(0, 0) + last_x.astype(F32) + last_one.astype(F32) + last_two.astype(F32)
    ).astype(LOW)

    parts = chosen_products(jnp.stack([number(offset) for offset in offsets]), mixed, weights)

    def tangent(offset):
        return parts[offsets.index(offset)].astype(F32)

    chain_a = step(add_rows(tangent(3), chain_a, 0).astype(LOW), "z", 1)
    chain_b = step(add_rows(tangent(-3), chain_b, half).astype(LOW), "z", -1)
    for offset in (2, 1):
        chain_a = step((tangent(offset) + chain_a.astype(F32)).astype(LOW), "z", 1)
        chain_b = step((tangent(-offset) + chain_b.astype(F32)).astype(LOW), "z", -1)
    total = tangent(0) + chain_a.astype(F32) + chain_b.astype(F32)
    left, right = total[:, :mine], total[:, mine:]
    of_own = jnp.where(first_core, left, right)
    of_other = jnp.where(first_core, right, left)
    sent = jnp.where(same, of_other, of_own).astype(LOW)
    near = lax.ppermute(sent, ("c", "xh"), [(1, 0), (2, 3), (0, 2), (3, 1)])
    cross = lax.ppermute(of_other.astype(LOW), ("c", "xh"), [(1, 2), (2, 1)])
    rest = jnp.where(same, of_own, cross.astype(F32))
    input_tangent = (rest + near.astype(F32)).astype(LOW).T
    return (curvature, input_tangent)


def solution(mesh):
    fine = Mesh(mesh.devices.reshape([SIZES[name] for name in AXES]), AXES)
    spec = P(("xl", "y", "c"), ("z", "xh"))
    return jax.shard_map(
        on_device, mesh=fine, in_specs=(spec,) * 7, out_specs=(spec, spec), check_vma=False
    )
```

```python
import jax
import jax.numpy as jnp
from jax import lax
from jax.experimental import pallas as pl
from jax.experimental.pallas import tpu as pltpu
from jax.sharding import Mesh, PartitionSpec as P

F32 = jnp.float32
LOW = jnp.bfloat16
SIZES = {"xl": 2, "y": 4, "c": 2, "z": 8, "xh": 2}
AXES = ("xl", "y", "c", "z", "xh")
VMEM = pl.BlockSpec(memory_space=pltpu.VMEM)
SMEM = pl.BlockSpec(memory_space=pltpu.SMEM)
ANY = pl.BlockSpec(memory_space=pl.ANY)


def swap(x, axis):
    return lax.ppermute(x, axis, [(0, 1), (1, 0)])


def step(x, axis, by):
    n = SIZES[axis]
    moves = [(c, i, (i + (by if c == 0 else -by)) % n) for c in range(2) for i in range(n)]
    if axis == "y":
        return lax.ppermute(x, ("y", "c"), [(2 * i + c, 2 * j + c) for c, i, j in moves])
    return lax.ppermute(x, ("c", "z"), [(n * c + i, n * c + j) for c, i, j in moves])


def after(*arrays):
    return lax.optimization_barrier(arrays)


def dot(left, right, dims):
    return lax.dot_general(left, right, (dims, ((), ())), preferred_element_type=F32)


def backward_kernel(kept, got, up_out, up_tangent, cotangent, cot_tangent, out):
    wide, room = up_out.shape[0], kept.shape[0] // 2
    rows = next(n for n in (96, 32, 16) if wide % n == 0)

    def body(i, carry):
        at = pl.ds(pl.multiple_of(i * rows, rows), rows)
        there = pl.ds(pl.multiple_of(i * rows + room, 16), rows)
        gate = kept[at, :] + got[at, :]
        gate_dot = kept[there, :] + got[there, :]
        sig = 1.0 / (1.0 + jnp.exp(-gate))
        first = sig * (1.0 + gate * (1.0 - sig))
        second = sig * (1.0 - sig) * (2.0 + gate * (1.0 - 2.0 * sig))
        up_val = up_out[at, :].astype(F32)
        cot_val = cotangent[at, :].astype(F32)
        up_dir = up_tangent[at, :].astype(F32)
        cot_dir = cot_tangent[at, :].astype(F32)
        both = cot_val * up_val
        out[there, :] = (both * first).astype(LOW)
        out[at, :] = (
            cot_dir * up_val * first + cot_val * up_dir * first + both * second * gate_dot
        ).astype(LOW)
        return carry

    lax.fori_loop(0, wide // rows, body, 0)
    if room > wide:
        gap = jnp.zeros((room - wide, out.shape[1]), LOW)
        out[wide:room, :] = gap
        out[room + wide:, :] = gap


def backward(kept, got, up_out, up_tangent, cotangent, cot_tangent):
    return pl.pallas_call(
        backward_kernel,
        out_shape=jax.ShapeDtypeStruct(kept.shape, LOW),
        in_specs=[VMEM] * 6,
        out_specs=VMEM,
        compiler_params=pltpu.CompilerParams(vmem_limit_bytes=24 * 2**20),
        cost_estimate=pl.CostEstimate(
            flops=20 * kept.size, bytes_accessed=14 * kept.size, transcendentals=kept.size // 2
        ),
    )(kept, got, up_out, up_tangent, cotangent, cot_tangent)


def products_kernel(order, right, other, *refs):
    blocks, out, held, sems = refs[:8], refs[8], refs[9], refs[10]
    count, columns = out.shape[0], right.shape[1]

    def fetch(i):
        for j, block in enumerate(blocks):
            @pl.when(order[i] == j)
            def _():
                pltpu.make_async_copy(block, held.at[i % 2], sems.at[i % 2]).start()

    fetch(0)

    def body(i, carry):
        @pl.when(i + 1 < count)
        def _():
            fetch(i + 1)

        pltpu.make_async_copy(blocks[0], held.at[i % 2], sems.at[i % 2]).wait()
        left = held[i % 2]
        out[i, :, :columns] = jnp.dot(left, right[...], preferred_element_type=F32).astype(LOW)
        out[i, :, columns:] = jnp.dot(left, other[...], preferred_element_type=F32).astype(LOW)
        return carry

    lax.fori_loop(0, count, body, 0)


def products(order, right, other, blocks):
    count, (rows, depth), columns = order.shape[0], blocks[0].shape, right.shape[1]
    return pl.pallas_call(
        products_kernel,
        out_shape=jax.ShapeDtypeStruct((count, rows, 2 * columns), LOW),
        in_specs=[SMEM, VMEM, VMEM] + [ANY] * 8,
        out_specs=VMEM,
        scratch_shapes=[pltpu.VMEM((2, rows, depth), LOW), pltpu.SemaphoreType.DMA((2,))],
        compiler_params=pltpu.CompilerParams(vmem_limit_bytes=24 * 2**20),
        cost_estimate=pl.CostEstimate(
            flops=4 * count * rows * depth * columns,
            bytes_accessed=2 * count * rows * (depth + columns),
            transcendentals=0,
        ),
    )(order, right, other, *blocks)


def add_rows(total, part, start):
    rows = part.shape[0]
    pieces = [total[start:start + rows] + part.astype(F32)]
    if start:
        pieces.insert(0, total[:start])
    if start + rows < total.shape[0]:
        pieces.append(total[start + rows:])
    return jnp.concatenate(pieces, axis=0)


def on_device(tokens, up_out, up_tangent, cotangent, cot_tangent, gate_weight, gate_direction):
    xl, y, c, z, xh = (lax.axis_index(name) for name in AXES)
    depth, wide = gate_weight.shape
    mine = tokens.shape[0]
    half = depth // 2
    same = c == xh
    sign = 1 - 2 * c

    room = -(-wide // 128) * 128
    gap = ((0, 0), (0, room - wide))
    own = jnp.concatenate([jnp.pad(gate_weight, gap), jnp.pad(gate_direction, gap)], axis=1)

    own, turned = after(own, tokens.T)
    near = lax.ppermute(turned, ("c", "xh"), [(2, 0), (1, 3), (0, 1), (3, 2)])
    cross = lax.ppermute(turned, ("c", "xh"), [(2, 1), (1, 2)])
    block = jnp.concatenate([jnp.where(same, turned, near), jnp.where(same, near, cross)], axis=1)

    one = step(own, "y", 1)
    two = step(own, "y", -1)
    over = swap(own, "xl")
    a1, b1 = step(block, "z", 1), step(block, "z", -1)
    one, two, a1, b1 = after(one, two, a1, b1)
    a2, b2 = step(a1, "z", 1), step(b1, "z", -1)
    far_one = step(one[:half], "y", 1)
    far_two = step(two[half:], "y", -1)
    a3, b3 = step(a2, "z", 1), step(b2, "z", -1)
    far = jnp.concatenate([far_one, far_two], axis=0)
    over, far = after(over, far)
    over_far = swap(far, "xl")
    over_one = step(over, "y", 1)
    over_two = step(over, "y", -1)
    a4, b4 = step(a3[:half], "z", 1), step(b3[half:], "z", -1)
    opposite = jnp.concatenate([a4, b4], axis=0)
    token_blocks = jnp.stack([block, b1, b2, b3, opposite, a3, a2, a1])
    weights = [own, two, far, one, over, over_two, over_far, over_one]

    def token_block(other, offset):
        place = jnp.bitwise_xor(xl, other) * 4 + (y + sign * offset + 4) % 4
        index = (sign * (place - z) + 16) % 8
        return lax.dynamic_index_in_dim(token_blocks, index, 0, keepdims=False)

    rows_of = [token_block(other, offset) for other in range(2) for offset in range(4)]
    kept = away = jnp.zeros((2 * room, mine), F32)
    for i in (0, 1, 3, 4, 2, 5, 7):
        kept = kept + dot(weights[i], rows_of[i][:, :mine], ((0,), (0,)))
        away = away + dot(weights[i], rows_of[i][:, mine:], ((0,), (0,)))
        kept, away = after(kept, away)
    away = away + dot(weights[6], rows_of[6][:, mine:], ((0,), (0,)))
    kept, away, last, last_rows = after(kept, away, weights[6], rows_of[6])
    got = swap(away, "c")
    kept = kept + dot(last, last_rows[:, :mine], ((0,), (0,)))

    mixed = backward(kept, got, up_out.T, up_tangent.T, cotangent.T, cot_tangent.T)
    other = swap(mixed, "c")

    def number(offset):
        place = (z + sign * offset + 8) % 8
        return jnp.bitwise_xor(place // 4, xl) * 4 + (sign * (place % 4 - y) + 8) % 4

    def tangents(*offsets):
        return products(jnp.stack([number(offset) for offset in offsets]), mixed, other, weights)

    opposite = tangents(4)[0]
    back_dot = jnp.concatenate([mixed[:wide], other[:wide]], axis=1)
    back_dot, opposite = after(back_dot, opposite)
    chain_a = step(opposite[:half], "z", 1)
    chain_b = step(opposite[half:], "z", -1)
    parts = tangents(3, -3, 2, -2, 1, -1, 0)
    sum_a = add_rows(parts[0].astype(F32), chain_a, 0).astype(LOW)
    sum_b = add_rows(parts[1].astype(F32), chain_b, half).astype(LOW)
    sum_a, sum_b, back_dot = after(sum_a, sum_b, back_dot)
    chain_a, chain_b = step(sum_a, "z", 1), step(sum_b, "z", -1)

    def curv(other, offset):
        return dot(rows_of[other * 4 + offset], back_dot, ((1,), (1,)))

    got_x = swap(curv(1, 2).astype(LOW), "xl")
    got_one = step(curv(1, 1).astype(LOW), "y", 1)
    got_two = step(curv(1, 3).astype(LOW), "y", -1)
    parts = [parts[i].astype(F32) for i in range(2, 7)]
    sum_a, sum_b = (parts[0] + chain_a.astype(F32)).astype(LOW), (parts[1] + chain_b.astype(F32)).astype(LOW)
    sum_a, sum_b = after(sum_a, sum_b)
    chain_a, chain_b = step(sum_a, "z", 1), step(sum_b, "z", -1)

    far_sum = (curv(0, 2) + got_x.astype(F32)).astype(LOW)
    far_one = step(far_sum[:half], "y", 1)
    far_two = step(far_sum[half:], "y", -1)
    sum_a, sum_b = (parts[2] + chain_a.astype(F32)).astype(LOW), (parts[3] + chain_b.astype(F32)).astype(LOW)
    sum_a, sum_b = after(sum_a, sum_b)
    chain_a, chain_b = step(sum_a, "z", 1), step(sum_b, "z", -1)

    over_sum = (curv(1, 0) + got_one.astype(F32) + got_two.astype(F32)).astype(LOW)
    last_x = swap(over_sum, "xl")
    last_one = step(add_rows(curv(0, 1), far_one, 0).astype(LOW), "y", 1)
    last_two = step(add_rows(curv(0, 3), far_two, half).astype(LOW), "y", -1)
    total = parts[4] + chain_a.astype(F32) + chain_b.astype(F32)
    of_own, of_other = total[:, :mine], total[:, mine:]
    sent = jnp.where(same, of_other, of_own).astype(LOW)
    near = lax.ppermute(sent, ("c", "xh"), [(1, 0), (2, 3), (0, 2), (3, 1)])
    cross = lax.ppermute(of_other.astype(LOW), ("c", "xh"), [(1, 2), (2, 1)])
    rest = jnp.where(same, of_own, cross.astype(F32))
    input_tangent = (rest + near.astype(F32)).astype(LOW).T

    curvature = (
        curv(0, 0) + last_x.astype(F32) + last_one.astype(F32) + last_two.astype(F32)
    ).astype(LOW)
    return (curvature, input_tangent)


def solution(mesh):
    fine = Mesh(mesh.devices.reshape([SIZES[name] for name in AXES]), AXES)
    spec = P(("xl", "y", "c"), ("z", "xh"))
    return jax.shard_map(
        on_device, mesh=fine, in_specs=(spec,) * 7, out_specs=(spec, spec), check_vma=False
    )
```

```python
import jax
import jax.numpy as jnp
from jax import lax
from jax.experimental import pallas as pl
from jax.experimental.pallas import tpu as pltpu
from jax.sharding import Mesh, PartitionSpec as P

F32 = jnp.float32
LOW = jnp.bfloat16
SIZES = {"xl": 2, "y": 4, "c": 2, "z": 8, "xh": 2}
AXES = ("xl", "y", "c", "z", "xh")
VMEM = pl.BlockSpec(memory_space=pltpu.VMEM)
SMEM = pl.BlockSpec(memory_space=pltpu.SMEM)
HBM = pl.BlockSpec(memory_space=pltpu.HBM)


def swap(x, axis):
    return lax.ppermute(x, axis, [(0, 1), (1, 0)])


def step(x, axis, by):
    n = SIZES[axis]
    moves = [(c, i, (i + (by if c == 0 else -by)) % n) for c in range(2) for i in range(n)]
    if axis == "y":
        return lax.ppermute(x, ("y", "c"), [(2 * i + c, 2 * j + c) for c, i, j in moves])
    return lax.ppermute(x, ("c", "z"), [(n * c + i, n * c + j) for c, i, j in moves])


def after(*arrays):
    return lax.optimization_barrier(arrays)


def dot(left, right, dims):
    return lax.dot_general(left, right, (dims, ((), ())), preferred_element_type=F32)


def backward_kernel(kept, got, up_out, up_tangent, cotangent, cot_tangent, out):
    wide, room = up_out.shape[0], kept.shape[0] // 2
    rows = next(n for n in (96, 32, 16) if wide % n == 0)

    def body(i, carry):
        at = pl.ds(pl.multiple_of(i * rows, rows), rows)
        there = pl.ds(pl.multiple_of(i * rows + room, 16), rows)
        gate = kept[at, :] + got[at, :]
        gate_dot = kept[there, :] + got[there, :]
        sig = 1.0 / (1.0 + jnp.exp(-gate))
        first = sig * (1.0 + gate * (1.0 - sig))
        second = sig * (1.0 - sig) * (2.0 + gate * (1.0 - 2.0 * sig))
        up_val = up_out[at, :].astype(F32)
        cot_val = cotangent[at, :].astype(F32)
        up_dir = up_tangent[at, :].astype(F32)
        cot_dir = cot_tangent[at, :].astype(F32)
        both = cot_val * up_val
        out[there, :] = (both * first).astype(LOW)
        out[at, :] = (
            cot_dir * up_val * first + cot_val * up_dir * first + both * second * gate_dot
        ).astype(LOW)
        return carry

    lax.fori_loop(0, wide // rows, body, 0)
    if room > wide:
        gap = jnp.zeros((room - wide, out.shape[1]), LOW)
        out[wide:room, :] = gap
        out[room + wide:, :] = gap


def backward(kept, got, up_out, up_tangent, cotangent, cot_tangent):
    return pl.pallas_call(
        backward_kernel,
        out_shape=jax.ShapeDtypeStruct(kept.shape, LOW),
        in_specs=[VMEM] * 6,
        out_specs=VMEM,
        compiler_params=pltpu.CompilerParams(vmem_limit_bytes=24 * 2**20),
        cost_estimate=pl.CostEstimate(
            flops=20 * kept.size, bytes_accessed=14 * kept.size, transcendentals=kept.size // 2
        ),
    )(kept, got, up_out, up_tangent, cotangent, cot_tangent)


def place_kernel(order, *refs):
    blocks, out, sems = refs[:8], refs[8], refs[9]
    copies = [
        pltpu.make_async_copy(block, out.at[order[j]], sems.at[j]) for j, block in enumerate(blocks)
    ]
    for copy in copies:
        copy.start()
    for copy in copies:
        copy.wait()


def place(order, blocks):
    shape = blocks[0].shape
    return pl.pallas_call(
        place_kernel,
        out_shape=jax.ShapeDtypeStruct((8,) + shape, LOW),
        in_specs=[SMEM] + [HBM] * 8,
        out_specs=VMEM,
        scratch_shapes=[pltpu.SemaphoreType.DMA((8,))],
        compiler_params=pltpu.CompilerParams(vmem_limit_bytes=24 * 2**20),
        cost_estimate=pl.CostEstimate(
            flops=0, bytes_accessed=32 * shape[0] * shape[1], transcendentals=0
        ),
    )(order, *blocks)


def add_rows(total, part, start):
    rows = part.shape[0]
    pieces = [total[start:start + rows] + part.astype(F32)]
    if start:
        pieces.insert(0, total[:start])
    if start + rows < total.shape[0]:
        pieces.append(total[start + rows:])
    return jnp.concatenate(pieces, axis=0)


def on_device(tokens, up_out, up_tangent, cotangent, cot_tangent, gate_weight, gate_direction):
    xl, y, c, z, xh = (lax.axis_index(name) for name in AXES)
    depth, wide = gate_weight.shape
    mine = tokens.shape[0]
    half = depth // 2
    same = c == xh
    sign = 1 - 2 * c

    room = -(-wide // 128) * 128
    gap = ((0, 0), (0, room - wide))
    own = jnp.concatenate([jnp.pad(gate_weight, gap), jnp.pad(gate_direction, gap)], axis=1)

    own, turned = after(own, tokens.T)
    near = lax.ppermute(turned, ("c", "xh"), [(2, 0), (1, 3), (0, 1), (3, 2)])
    cross = lax.ppermute(turned, ("c", "xh"), [(2, 1), (1, 2)])
    block = jnp.concatenate([jnp.where(same, turned, near), jnp.where(same, near, cross)], axis=1)

    one = step(own, "y", 1)
    over = swap(own, "xl")
    later, block = after(own, block)
    two = step(later, "y", -1)
    a1, b1 = step(block, "z", 1), step(block, "z", -1)
    one, a1, b1 = after(one, a1, b1)
    a2, b2 = step(a1, "z", 1), step(b1, "z", -1)
    far_one = step(one[:half], "y", 1)
    a3, b3 = step(a2, "z", 1), step(b2, "z", -1)
    far_two = step(two[half:], "y", -1)
    a4, b4 = step(a3[:half], "z", 1), step(b3[half:], "z", -1)
    over, far_one = after(over, far_one)
    over_one = step(over, "y", 1)
    over, far_two = after(over, far_two)
    far = jnp.concatenate([far_one, far_two], axis=0)
    over_far = swap(far, "xl")
    over_two = step(over, "y", -1)
    opposite = jnp.concatenate([a4, b4], axis=0)
    token_blocks = jnp.stack([block, b1, b2, b3, opposite, a3, a2, a1])
    weights = [own, two, far, one, over, over_two, over_far, over_one]

    index = jnp.stack([
        (sign * (jnp.bitwise_xor(xl, j // 4) * 4 + (y + sign * j + 8) % 4 - z) + 16) % 8
        for j in range(8)
    ])
    rows_of = [
        lax.dynamic_index_in_dim(token_blocks, index[j], 0, keepdims=False) for j in range(8)
    ]
    kept = away = jnp.zeros((2 * room, mine), F32)
    for i in (0, 1, 3, 4, 2, 5, 7):
        kept = kept + dot(weights[i], rows_of[i][:, :mine], ((0,), (0,)))
        away = away + dot(weights[i], rows_of[i][:, mine:], ((0,), (0,)))
        kept, away = after(kept, away)
    away = away + dot(weights[6], rows_of[6][:, mine:], ((0,), (0,)))
    kept, away, last, last_rows = after(kept, away, weights[6], rows_of[6])
    got = swap(away, "c")
    along = place(index, weights)
    got, along = after(got, along)
    kept = kept + dot(last, last_rows[:, :mine], ((0,), (0,)))

    mixed = backward(kept, got, up_out.T, up_tangent.T, cotangent.T, cot_tangent.T)
    other = swap(mixed, "c")

    everyone = jnp.concatenate([mixed, other], axis=1)

    def tangent(offset):
        return dot(along[offset % 8], everyone, ((1,), (0,)))

    opposite = tangent(4).astype(LOW)
    chain_a = step(opposite[:half], "z", 1)
    chain_b = step(opposite[half:], "z", -1)
    sum_a = add_rows(tangent(3), chain_a, 0).astype(LOW)
    chain_a = step(sum_a, "z", 1)
    sum_b = add_rows(tangent(-3), chain_b, half).astype(LOW)
    back_dot, sum_b = after(everyone[:wide], sum_b)
    chain_b = step(sum_b, "z", -1)

    def curv(other, offset):
        return dot(rows_of[other * 4 + offset], back_dot, ((1,), (1,)))

    got_x = swap(curv(1, 2).astype(LOW), "xl")
    got_one = step(curv(1, 1).astype(LOW), "y", 1)
    got_two = step(curv(1, 3).astype(LOW), "y", -1)
    chain_a = step((tangent(2) + chain_a.astype(F32)).astype(LOW), "z", 1)
    chain_b = step((tangent(-2) + chain_b.astype(F32)).astype(LOW), "z", -1)

    far_sum = (curv(0, 2) + got_x.astype(F32)).astype(LOW)
    far_one = step(far_sum[:half], "y", 1)
    far_two = step(far_sum[half:], "y", -1)
    chain_a = step((tangent(1) + chain_a.astype(F32)).astype(LOW), "z", 1)
    chain_b = step((tangent(-1) + chain_b.astype(F32)).astype(LOW), "z", -1)

    over_sum = (curv(1, 0) + got_one.astype(F32) + got_two.astype(F32)).astype(LOW)
    last_x = swap(over_sum, "xl")
    last_one = step(add_rows(curv(0, 1), far_one, 0).astype(LOW), "y", 1)
    last_two = step(add_rows(curv(0, 3), far_two, half).astype(LOW), "y", -1)
    total = tangent(0) + chain_a.astype(F32) + chain_b.astype(F32)
    of_own, of_other = total[:, :mine], total[:, mine:]
    sent = jnp.where(same, of_other, of_own).astype(LOW)
    near = lax.ppermute(sent, ("c", "xh"), [(1, 0), (2, 3), (0, 2), (3, 1)])
    cross = lax.ppermute(of_other.astype(LOW), ("c", "xh"), [(1, 2), (2, 1)])
    rest = jnp.where(same, of_own, cross.astype(F32))
    input_tangent = (rest + near.astype(F32)).astype(LOW).T

    curvature = (
        curv(0, 0) + last_x.astype(F32) + last_one.astype(F32) + last_two.astype(F32)
    ).astype(LOW)
    return (curvature, input_tangent)


def solution(mesh):
    fine = Mesh(mesh.devices.reshape([SIZES[name] for name in AXES]), AXES)
    spec = P(("xl", "y", "c"), ("z", "xh"))
    return jax.shard_map(
        on_device, mesh=fine, in_specs=(spec,) * 7, out_specs=(spec, spec), check_vma=False
    )
```

```python
import functools

import jax
import jax.numpy as jnp
from jax import lax
from jax.experimental import pallas as pl
from jax.experimental.pallas import tpu as pltpu
from jax.sharding import Mesh, PartitionSpec as P

F32 = jnp.float32
LOW = jnp.bfloat16
SIZES = {"xl": 2, "y": 4, "c": 2, "z": 8, "xh": 2}
AXES = ("xl", "y", "c", "z", "xh")
VMEM = pl.BlockSpec(memory_space=pltpu.VMEM)
SMEM = pl.BlockSpec(memory_space=pltpu.SMEM)
ANY = pl.BlockSpec(memory_space=pl.ANY)


def swap(x, axis):
    return lax.ppermute(x, axis, [(0, 1), (1, 0)])


def step(x, axis, by):
    n = SIZES[axis]
    moves = [(c, i, (i + (by if c == 0 else -by)) % n) for c in range(2) for i in range(n)]
    if axis == "y":
        return lax.ppermute(x, ("y", "c"), [(2 * i + c, 2 * j + c) for c, i, j in moves])
    return lax.ppermute(x, ("c", "z"), [(n * c + i, n * c + j) for c, i, j in moves])


def after(*arrays):
    return lax.optimization_barrier(arrays)


def dot(left, right, dims):
    return lax.dot_general(left, right, (dims, ((), ())), preferred_element_type=F32)


def backward_kernel(kept, got, up_out, up_tangent, cotangent, cot_tangent, out):
    wide, room = up_out.shape[0], kept.shape[0] // 2
    rows = next(n for n in (96, 32, 16) if wide % n == 0)

    def body(i, carry):
        at = pl.ds(pl.multiple_of(i * rows, rows), rows)
        there = pl.ds(pl.multiple_of(i * rows + room, 16), rows)
        gate = kept[at, :] + got[at, :].astype(F32)
        gate_dot = kept[there, :] + got[there, :].astype(F32)
        sig = 1.0 / (1.0 + jnp.exp(-gate))
        first = sig * (1.0 + gate * (1.0 - sig))
        second = sig * (1.0 - sig) * (2.0 + gate * (1.0 - 2.0 * sig))
        up_val = up_out[at, :].astype(F32)
        cot_val = cotangent[at, :].astype(F32)
        up_dir = up_tangent[at, :].astype(F32)
        cot_dir = cot_tangent[at, :].astype(F32)
        both = cot_val * up_val
        out[there, :] = (both * first).astype(LOW)
        out[at, :] = (
            cot_dir * up_val * first + cot_val * up_dir * first + both * second * gate_dot
        ).astype(LOW)
        return carry

    lax.fori_loop(0, wide // rows, body, 0)
    if room > wide:
        gap = jnp.zeros((room - wide, out.shape[1]), LOW)
        out[wide:room, :] = gap
        out[room + wide:, :] = gap


def backward(kept, got, up_out, up_tangent, cotangent, cot_tangent):
    return pl.pallas_call(
        backward_kernel,
        out_shape=jax.ShapeDtypeStruct(kept.shape, LOW),
        in_specs=[VMEM] * 6,
        out_specs=VMEM,
        compiler_params=pltpu.CompilerParams(vmem_limit_bytes=24 * 2**20),
        cost_estimate=pl.CostEstimate(
            flops=20 * kept.size, bytes_accessed=14 * kept.size, transcendentals=kept.size // 2
        ),
    )(kept, got, up_out, up_tangent, cotangent, cot_tangent)


def place_kernel(spots, order, *refs):
    pieces, out, sems = refs[:len(spots)], refs[-2], refs[-1]
    copies = [
        pltpu.make_async_copy(
            piece, out.at[order[j], pl.ds(row, piece.shape[0])], sems.at[i]
        )
        for i, (piece, (j, row)) in enumerate(zip(pieces, spots))
    ]
    for copy in copies:
        copy.start()
    for copy in copies:
        copy.wait()


def place(order, spots, pieces, rows, into=None):
    columns = pieces[0].shape[1]
    extra = [] if into is None else [into]
    return pl.pallas_call(
        functools.partial(place_kernel, spots),
        out_shape=jax.ShapeDtypeStruct((8, rows, columns), LOW),
        in_specs=[SMEM] + [ANY] * (len(pieces) + len(extra)),
        out_specs=ANY,
        input_output_aliases={1 + len(pieces): 0} if extra else {},
        scratch_shapes=[pltpu.SemaphoreType.DMA((len(pieces),))],
        compiler_params=pltpu.CompilerParams(vmem_limit_bytes=24 * 2**20),
        cost_estimate=pl.CostEstimate(
            flops=0, bytes_accessed=4 * sum(p.size for p in pieces), transcendentals=0
        ),
    )(order, *pieces, *extra)


def add_rows(total, part, start):
    rows = part.shape[0]
    pieces = [total[start:start + rows] + part.astype(F32)]
    if start:
        pieces.insert(0, total[:start])
    if start + rows < total.shape[0]:
        pieces.append(total[start + rows:])
    return jnp.concatenate(pieces, axis=0)


def on_device(tokens, up_out, up_tangent, cotangent, cot_tangent, gate_weight, gate_direction):
    xl, y, c, z, xh = (lax.axis_index(name) for name in AXES)
    depth, wide = gate_weight.shape
    mine = tokens.shape[0]
    half = depth // 2
    same = c == xh
    sign = 1 - 2 * c

    room = -(-wide // 128) * 128
    gap = ((0, 0), (0, room - wide))
    own = jnp.concatenate([jnp.pad(gate_weight, gap), jnp.pad(gate_direction, gap)], axis=1)

    own, turned = after(own, tokens.T)
    near = lax.ppermute(turned, ("c", "xh"), [(2, 0), (1, 3), (0, 1), (3, 2)])
    cross = lax.ppermute(turned, ("c", "xh"), [(2, 1), (1, 2)])
    block = jnp.concatenate([jnp.where(same, turned, near), jnp.where(same, near, cross)], axis=1)

    one = step(own, "y", 1)
    over = swap(own, "xl")
    later, block = after(own, block)
    two = step(later, "y", -1)
    a1, b1 = step(block, "z", 1), step(block, "z", -1)
    one, a1, b1 = after(one, a1, b1)
    a2, b2 = step(a1, "z", 1), step(b1, "z", -1)
    far_one = step(one[:half], "y", 1)
    a3, b3 = step(a2, "z", 1), step(b2, "z", -1)
    far_two = step(two[half:], "y", -1)
    a4, b4 = step(a3[:half], "z", 1), step(b3[half:], "z", -1)
    over, far_one = after(over, far_one)
    over_far_one = swap(far_one, "xl")
    over_one = step(over, "y", 1)
    over, far_two = after(over, far_two)
    over_far_two = swap(far_two, "xl")
    over_two = step(over, "y", -1)
    opposite = jnp.concatenate([a4, b4], axis=0)
    token_blocks = jnp.stack([block, b1, b2, b3, opposite, a3, a2, a1])

    index = jnp.stack([
        (sign * (jnp.bitwise_xor(xl, j // 4) * 4 + (y + sign * j + 8) % 4 - z) + 16) % 8
        for j in range(8)
    ])
    rows_of = [
        lax.dynamic_index_in_dim(token_blocks, index[j], 0, keepdims=False) for j in range(8)
    ]
    early = [(own, 0, 0), (over, 4, 0), (one, 3, 0), (two, 1, 0), (far_one, 2, 0), (far_two, 2, half)]
    late = [(over_far_one, 6, 0), (over_one, 7, 0), (over_far_two, 6, half), (over_two, 5, 0)]
    kept = away = jnp.zeros((2 * room, mine), F32)
    along = None
    for group in (early, late):
        for piece, j, row in group:
            rows = rows_of[j][row:row + piece.shape[0]]
            kept, away, piece, rows = after(kept, away, piece, rows)
            away = away + dot(piece, rows[:, mine:], ((0,), (0,)))
            if (j, row) != (5, 0):
                kept = kept + dot(piece, rows[:, :mine], ((0,), (0,)))
        if group is early:
            spots, pieces = [g[1:] for g in group], [g[0] for g in group]
            along = place(index, spots, pieces, depth)
            along, kept = after(along, kept)
    got = swap(away.astype(LOW), "c")
    kept = kept + dot(piece, rows[:, :mine], ((0,), (0,)))
    spots, pieces = [g[1:] for g in late], [g[0] for g in late]
    along = place(index, spots, pieces, depth, along)
    got, along = after(got, along)

    mixed = backward(kept, got, up_out.T, up_tangent.T, cotangent.T, cot_tangent.T)
    other = swap(mixed, "c")

    everyone = jnp.concatenate([mixed, other], axis=1)

    def tangent(offset):
        return dot(along[offset % 8], everyone, ((1,), (0,)))

    opposite = tangent(4).astype(LOW)
    chain_a = step(opposite[:half], "z", 1)
    chain_b = step(opposite[half:], "z", -1)
    sum_a = add_rows(tangent(3), chain_a, 0).astype(LOW)
    sum_b = add_rows(tangent(-3), chain_b, half).astype(LOW)
    back_dot, sum_b = after(everyone[:wide], sum_b)

    def curv(other, offset):
        return dot(rows_of[other * 4 + offset], back_dot, ((1,), (1,)))

    to_x, to_one, to_two = (curv(1, i).astype(LOW) for i in (2, 1, 3))
    got_x = swap(to_x, "xl")
    got_one = step(to_one, "y", 1)
    got_two = step(to_two, "y", -1)
    chain_a, chain_b = step(sum_a, "z", 1), step(sum_b, "z", -1)
    sum_a = (tangent(2) + chain_a.astype(F32)).astype(LOW)
    sum_b = (tangent(-2) + chain_b.astype(F32)).astype(LOW)
    chain_a, chain_b = step(sum_a, "z", 1), step(sum_b, "z", -1)

    got_x, got_one, got_two, sum_b = after(got_x, got_one, got_two, sum_b)
    far_sum = (curv(0, 2) + got_x.astype(F32)).astype(LOW)
    far_one = step(far_sum[:half], "y", 1)
    far_two = step(far_sum[half:], "y", -1)
    over_sum = (curv(1, 0) + got_one.astype(F32) + got_two.astype(F32)).astype(LOW)
    last_x = swap(over_sum, "xl")
    sum_a = (tangent(1) + chain_a.astype(F32)).astype(LOW)
    sum_b = (tangent(-1) + chain_b.astype(F32)).astype(LOW)
    chain_a, chain_b = step(sum_a, "z", 1), step(sum_b, "z", -1)

    far_one, far_two, sum_b = after(far_one, far_two, sum_b)
    last_one = step(add_rows(curv(0, 1), far_one, 0).astype(LOW), "y", 1)
    last_two = step(add_rows(curv(0, 3), far_two, half).astype(LOW), "y", -1)
    total = tangent(0) + chain_a.astype(F32) + chain_b.astype(F32)
    of_own, of_other = total[:, :mine], total[:, mine:]
    sent = jnp.where(same, of_other, of_own).astype(LOW)
    near = lax.ppermute(sent, ("c", "xh"), [(1, 0), (2, 3), (0, 2), (3, 1)])
    cross = lax.ppermute(of_other.astype(LOW), ("c", "xh"), [(1, 2), (2, 1)])
    rest = jnp.where(same, of_own, cross.astype(F32))
    input_tangent = (rest + near.astype(F32)).astype(LOW).T

    curvature = (
        curv(0, 0) + last_x.astype(F32) + last_one.astype(F32) + last_two.astype(F32)
    ).astype(LOW)
    return (curvature, input_tangent)


def solution(mesh):
    fine = Mesh(mesh.devices.reshape([SIZES[name] for name in AXES]), AXES)
    spec = P(("xl", "y", "c"), ("z", "xh"))
    return jax.shard_map(
        on_device, mesh=fine, in_specs=(spec,) * 7, out_specs=(spec, spec), check_vma=False
    )
```

```python
import functools

import jax
import jax.numpy as jnp
from jax import lax
from jax.experimental import pallas as pl
from jax.experimental.pallas import tpu as pltpu
from jax.sharding import Mesh, PartitionSpec as P

F32 = jnp.float32
LOW = jnp.bfloat16
SIZES = {"xl": 2, "y": 4, "c": 2, "z": 8, "xh": 2}
AXES = ("xl", "y", "c", "z", "xh")
VMEM = pl.BlockSpec(memory_space=pltpu.VMEM)
SMEM = pl.BlockSpec(memory_space=pltpu.SMEM)
ANY = pl.BlockSpec(memory_space=pl.ANY)


def swap(x, axis):
    return lax.ppermute(x, axis, [(0, 1), (1, 0)])


def step(x, axis, by):
    n = SIZES[axis]
    moves = [(c, i, (i + (by if c == 0 else -by)) % n) for c in range(2) for i in range(n)]
    if axis == "y":
        return lax.ppermute(x, ("y", "c"), [(2 * i + c, 2 * j + c) for c, i, j in moves])
    return lax.ppermute(x, ("c", "z"), [(n * c + i, n * c + j) for c, i, j in moves])


def after(*arrays):
    return lax.optimization_barrier(arrays)


def dot(left, right, dims):
    return lax.dot_general(left, right, (dims, ((), ())), preferred_element_type=F32)


def backward_kernel(kept, got, up_out, up_tangent, cotangent, cot_tangent, out):
    wide, room = up_out.shape[0], kept.shape[0] // 2
    rows = next(n for n in (96, 32, 16) if wide % n == 0)

    def body(i, carry):
        at = pl.ds(pl.multiple_of(i * rows, rows), rows)
        there = pl.ds(pl.multiple_of(i * rows + room, 16), rows)
        gate = kept[at, :] + got[at, :].astype(F32)
        gate_dot = kept[there, :] + got[there, :].astype(F32)
        sig = 1.0 / (1.0 + jnp.exp(-gate))
        first = sig * (1.0 + gate * (1.0 - sig))
        second = sig * (1.0 - sig) * (2.0 + gate * (1.0 - 2.0 * sig))
        up_val = up_out[at, :].astype(F32)
        cot_val = cotangent[at, :].astype(F32)
        up_dir = up_tangent[at, :].astype(F32)
        cot_dir = cot_tangent[at, :].astype(F32)
        both = cot_val * up_val
        out[there, :] = (both * first).astype(LOW)
        out[at, :] = (
            cot_dir * up_val * first + cot_val * up_dir * first + both * second * gate_dot
        ).astype(LOW)
        return carry

    lax.fori_loop(0, wide // rows, body, 0)
    if room > wide:
        gap = jnp.zeros((room - wide, out.shape[1]), LOW)
        out[wide:room, :] = gap
        out[room + wide:, :] = gap


def backward(kept, got, up_out, up_tangent, cotangent, cot_tangent):
    return pl.pallas_call(
        backward_kernel,
        out_shape=jax.ShapeDtypeStruct(kept.shape, LOW),
        in_specs=[VMEM] * 6,
        out_specs=VMEM,
        compiler_params=pltpu.CompilerParams(vmem_limit_bytes=24 * 2**20),
        cost_estimate=pl.CostEstimate(
            flops=20 * kept.size, bytes_accessed=14 * kept.size, transcendentals=kept.size // 2
        ),
    )(kept, got, up_out, up_tangent, cotangent, cot_tangent)


def gate_kernel(count, *refs):
    pieces, rows, kept, away = refs[:count], refs[count:-2], refs[-2], refs[-1]
    mine = kept.shape[1]
    tile = next(n for n in (256, 128, 64) if kept.shape[0] % n == 0)

    def body(i, carry):
        at = pl.ds(pl.multiple_of(i * tile, tile), tile)
        total = None
        for piece, row in zip(pieces, rows):
            part = dot(piece[:, at], row[...], ((0,), (0,)))
            total = part if total is None else total + part
        kept[at, :] = total[:, :mine]
        away[at, :] = total[:, mine:]
        return carry

    lax.fori_loop(0, kept.shape[0] // tile, body, 0)


def gate_products(pieces, rows):
    columns, mine = pieces[0].shape[1], rows[0].shape[1] // 2
    depth = sum(p.shape[0] for p in pieces)
    return pl.pallas_call(
        functools.partial(gate_kernel, len(pieces)),
        out_shape=(jax.ShapeDtypeStruct((columns, mine), F32),) * 2,
        in_specs=[VMEM] * (2 * len(pieces)),
        out_specs=(VMEM, VMEM),
        compiler_params=pltpu.CompilerParams(vmem_limit_bytes=24 * 2**20),
        cost_estimate=pl.CostEstimate(
            flops=4 * depth * columns * mine,
            bytes_accessed=2 * depth * (columns + 2 * mine) + 8 * columns * mine,
            transcendentals=0,
        ),
    )(*pieces, *rows)


def place_kernel(spots, order, *refs):
    pieces, out, sems = refs[:len(spots)], refs[-2], refs[-1]
    copies = [
        pltpu.make_async_copy(
            piece, out.at[order[j], pl.ds(row, piece.shape[0])], sems.at[i]
        )
        for i, (piece, (j, row)) in enumerate(zip(pieces, spots))
    ]
    for copy in copies:
        copy.start()
    for copy in copies:
        copy.wait()


def place(order, spots, pieces, rows, into=None):
    columns = pieces[0].shape[1]
    extra = [] if into is None else [into]
    return pl.pallas_call(
        functools.partial(place_kernel, spots),
        out_shape=jax.ShapeDtypeStruct((8, rows, columns), LOW),
        in_specs=[SMEM] + [ANY] * (len(pieces) + len(extra)),
        out_specs=ANY,
        input_output_aliases={1 + len(pieces): 0} if extra else {},
        scratch_shapes=[pltpu.SemaphoreType.DMA((len(pieces),))],
        compiler_params=pltpu.CompilerParams(vmem_limit_bytes=24 * 2**20),
        cost_estimate=pl.CostEstimate(
            flops=0, bytes_accessed=4 * sum(p.size for p in pieces), transcendentals=0
        ),
    )(order, *pieces, *extra)


def add_rows(total, part, start):
    rows = part.shape[0]
    pieces = [total[start:start + rows] + part.astype(F32)]
    if start:
        pieces.insert(0, total[:start])
    if start + rows < total.shape[0]:
        pieces.append(total[start + rows:])
    return jnp.concatenate(pieces, axis=0)


def on_device(tokens, up_out, up_tangent, cotangent, cot_tangent, gate_weight, gate_direction):
    xl, y, c, z, xh = (lax.axis_index(name) for name in AXES)
    depth, wide = gate_weight.shape
    mine = tokens.shape[0]
    half = depth // 2
    same = c == xh
    sign = 1 - 2 * c

    room = -(-wide // 128) * 128
    gap = ((0, 0), (0, room - wide))
    own = jnp.concatenate([jnp.pad(gate_weight, gap), jnp.pad(gate_direction, gap)], axis=1)

    own, turned = after(own, tokens.T)
    near = lax.ppermute(turned, ("c", "xh"), [(2, 0), (1, 3), (0, 1), (3, 2)])
    cross = lax.ppermute(turned, ("c", "xh"), [(2, 1), (1, 2)])
    block = jnp.concatenate([jnp.where(same, turned, near), jnp.where(same, near, cross)], axis=1)

    one = step(own, "y", 1)
    over = swap(own, "xl")
    later, block = after(own, block)
    two = step(later, "y", -1)
    a1, b1 = step(block, "z", 1), step(block, "z", -1)
    a2, b2 = step(a1, "z", 1), step(b1, "z", -1)
    one, a2, b2 = after(one, a2, b2)
    far_one = step(one[:half], "y", 1)
    a3, b3 = step(a2, "z", 1), step(b2, "z", -1)
    far_two = step(two[half:], "y", -1)
    far_one, over, a3, b3 = after(far_one, over, a3, b3)
    a4, b4 = step(a3[:half], "z", 1), step(b3[half:], "z", -1)
    over, far_one = after(over, far_one)
    over_far_one = swap(far_one, "xl")
    over_one = step(over, "y", 1)
    over, far_two = after(over, far_two)
    over_far_two = swap(far_two, "xl")
    over_two = step(over, "y", -1)
    opposite = jnp.concatenate([a4, b4], axis=0)
    token_blocks = jnp.stack([block, b1, b2, b3, opposite, a3, a2, a1])

    index = jnp.stack([
        (sign * (jnp.bitwise_xor(xl, j // 4) * 4 + (y + sign * j + 8) % 4 - z) + 16) % 8
        for j in range(8)
    ])
    rows_of = [
        lax.dynamic_index_in_dim(token_blocks, index[j], 0, keepdims=False) for j in range(8)
    ]
    early = [(own, 0, 0), (over, 4, 0), (one, 3, 0), (two, 1, 0), (far_one, 2, 0), (far_two, 2, half)]
    late = [(over_far_one, 6, 0), (over_one, 7, 0), (over_far_two, 6, half), (over_two, 5, 0)]
    spots, pieces = [g[1:] for g in early], [g[0] for g in early]
    along = place(index, spots, pieces, depth)
    kept, away = gate_products(
        pieces, [rows_of[j][row:row + piece.shape[0]] for piece, j, row in early]
    )
    along, kept = after(along, kept)
    for piece, j, row in late:
        rows = rows_of[j][row:row + piece.shape[0]]
        kept, away, piece, rows = after(kept, away, piece, rows)
        away = away + dot(piece, rows[:, mine:], ((0,), (0,)))
        if j != 5:
            kept = kept + dot(piece, rows[:, :mine], ((0,), (0,)))
    got = swap(away.astype(LOW), "c")
    kept = kept + dot(piece, rows[:, :mine], ((0,), (0,)))
    spots, pieces = [g[1:] for g in late], [g[0] for g in late]
    along = place(index, spots, pieces, depth, along)
    got, along = after(got, along)

    mixed = backward(kept, got, up_out.T, up_tangent.T, cotangent.T, cot_tangent.T)
    other = swap(mixed, "c")

    everyone = jnp.concatenate([mixed, other], axis=1)

    def tangent(offset):
        return dot(along[offset % 8], everyone, ((1,), (0,)))

    opposite = tangent(4).astype(LOW)
    chain_a = step(opposite[:half], "z", 1)
    chain_b = step(opposite[half:], "z", -1)
    back_dot = everyone[:wide]

    def curv(other, offset):
        return dot(rows_of[other * 4 + offset], back_dot, ((1,), (1,)))

    to_x, to_one, to_two = (curv(1, i).astype(LOW) for i in (2, 1, 3))
    sum_a = add_rows(tangent(3), chain_a, 0).astype(LOW)
    sum_b = add_rows(tangent(-3), chain_b, half).astype(LOW)
    got_x = swap(to_x, "xl")
    got_one = step(to_one, "y", 1)
    got_two = step(to_two, "y", -1)
    chain_a, chain_b = step(sum_a, "z", 1), step(sum_b, "z", -1)
    sum_a = (tangent(2) + chain_a.astype(F32)).astype(LOW)
    sum_b = (tangent(-2) + chain_b.astype(F32)).astype(LOW)
    got_x, got_one, got_two, sum_a, sum_b = after(got_x, got_one, got_two, sum_a, sum_b)
    chain_a, chain_b = step(sum_a, "z", 1), step(sum_b, "z", -1)

    far_sum = (curv(0, 2) + got_x.astype(F32)).astype(LOW)
    far_one = step(far_sum[:half], "y", 1)
    far_two = step(far_sum[half:], "y", -1)
    over_sum = (curv(1, 0) + got_one.astype(F32) + got_two.astype(F32)).astype(LOW)
    last_x = swap(over_sum, "xl")
    sum_a = (tangent(1) + chain_a.astype(F32)).astype(LOW)
    sum_b = (tangent(-1) + chain_b.astype(F32)).astype(LOW)
    far_one, far_two, sum_a, sum_b = after(far_one, far_two, sum_a, sum_b)
    chain_a, chain_b = step(sum_a, "z", 1), step(sum_b, "z", -1)

    last_one = step(add_rows(curv(0, 1), far_one, 0).astype(LOW), "y", 1)
    last_two = step(add_rows(curv(0, 3), far_two, half).astype(LOW), "y", -1)
    total = tangent(0) + chain_a.astype(F32) + chain_b.astype(F32)
    of_own, of_other = total[:, :mine], total[:, mine:]
    sent = jnp.where(same, of_other, of_own).astype(LOW)
    near = lax.ppermute(sent, ("c", "xh"), [(1, 0), (2, 3), (0, 2), (3, 1)])
    cross = lax.ppermute(of_other.astype(LOW), ("c", "xh"), [(1, 2), (2, 1)])
    rest = jnp.where(same, of_own, cross.astype(F32))
    input_tangent = (rest + near.astype(F32)).astype(LOW).T

    curvature = (
        curv(0, 0) + last_x.astype(F32) + last_one.astype(F32) + last_two.astype(F32)
    ).astype(LOW)
    return (curvature, input_tangent)


def solution(mesh):
    fine = Mesh(mesh.devices.reshape([SIZES[name] for name in AXES]), AXES)
    spec = P(("xl", "y", "c"), ("z", "xh"))
    return jax.shard_map(
        on_device, mesh=fine, in_specs=(spec,) * 7, out_specs=(spec, spec), check_vma=False
    )
```

```python
import functools

import jax
import jax.numpy as jnp
from jax import lax
from jax.experimental import pallas as pl
from jax.experimental.pallas import tpu as pltpu
from jax.sharding import Mesh, PartitionSpec as P

F32 = jnp.float32
LOW = jnp.bfloat16
SIZES = {"xl": 2, "y": 4, "c": 2, "z": 8, "xh": 2}
AXES = ("xl", "y", "c", "z", "xh")
VMEM = pl.BlockSpec(memory_space=pltpu.VMEM)
SMEM = pl.BlockSpec(memory_space=pltpu.SMEM)
ANY = pl.BlockSpec(memory_space=pl.ANY)


def swap(x, axis):
    return lax.ppermute(x, axis, [(0, 1), (1, 0)])


def step(x, axis, by):
    n = SIZES[axis]
    moves = [(c, i, (i + (by if c == 0 else -by)) % n) for c in range(2) for i in range(n)]
    if axis == "y":
        return lax.ppermute(x, ("y", "c"), [(2 * i + c, 2 * j + c) for c, i, j in moves])
    return lax.ppermute(x, ("c", "z"), [(n * c + i, n * c + j) for c, i, j in moves])


def after(*arrays):
    return lax.optimization_barrier(arrays)


def dot(left, right, dims):
    return lax.dot_general(left, right, (dims, ((), ())), preferred_element_type=F32)


def backward_kernel(kept, got, up_out, up_tangent, cotangent, cot_tangent, out):
    wide, room = up_out.shape[0], kept.shape[0] // 2
    rows = next(n for n in (96, 32, 16) if wide % n == 0)

    def body(i, carry):
        at = pl.ds(pl.multiple_of(i * rows, rows), rows)
        there = pl.ds(pl.multiple_of(i * rows + room, 16), rows)
        gate = kept[at, :] + got[at, :].astype(F32)
        gate_dot = kept[there, :] + got[there, :].astype(F32)
        sig = 1.0 / (1.0 + jnp.exp(-gate))
        first = sig * (1.0 + gate * (1.0 - sig))
        second = sig * (1.0 - sig) * (2.0 + gate * (1.0 - 2.0 * sig))
        up_val = up_out[at, :].astype(F32)
        cot_val = cotangent[at, :].astype(F32)
        up_dir = up_tangent[at, :].astype(F32)
        cot_dir = cot_tangent[at, :].astype(F32)
        both = cot_val * up_val
        out[there, :] = (both * first).astype(LOW)
        out[at, :] = (
            cot_dir * up_val * first + cot_val * up_dir * first + both * second * gate_dot
        ).astype(LOW)
        return carry

    lax.fori_loop(0, wide // rows, body, 0)
    if room > wide:
        gap = jnp.zeros((room - wide, out.shape[1]), LOW)
        out[wide:room, :] = gap
        out[room + wide:, :] = gap


def backward(kept, got, up_out, up_tangent, cotangent, cot_tangent):
    return pl.pallas_call(
        backward_kernel,
        out_shape=jax.ShapeDtypeStruct(kept.shape, LOW),
        in_specs=[VMEM] * 6,
        out_specs=VMEM,
        compiler_params=pltpu.CompilerParams(vmem_limit_bytes=24 * 2**20),
        cost_estimate=pl.CostEstimate(
            flops=20 * kept.size, bytes_accessed=14 * kept.size, transcendentals=kept.size // 2
        ),
    )(kept, got, up_out, up_tangent, cotangent, cot_tangent)


def gate_kernel(count, *refs):
    pieces, rows, kept, away = refs[:count], refs[count:-2], refs[-2], refs[-1]
    mine = kept.shape[1]
    tile = next(n for n in (256, 128, 64) if kept.shape[0] % n == 0)

    def body(i, carry):
        at = pl.ds(pl.multiple_of(i * tile, tile), tile)
        total = None
        for piece, row in zip(pieces, rows):
            part = dot(piece[:, at], row[...], ((0,), (0,)))
            total = part if total is None else total + part
        kept[at, :] = total[:, :mine]
        away[at, :] = total[:, mine:]
        return carry

    lax.fori_loop(0, kept.shape[0] // tile, body, 0)


def gate_products(pieces, rows):
    columns, mine = pieces[0].shape[1], rows[0].shape[1] // 2
    depth = sum(p.shape[0] for p in pieces)
    return pl.pallas_call(
        functools.partial(gate_kernel, len(pieces)),
        out_shape=(jax.ShapeDtypeStruct((columns, mine), F32),) * 2,
        in_specs=[VMEM] * (2 * len(pieces)),
        out_specs=(VMEM, VMEM),
        compiler_params=pltpu.CompilerParams(vmem_limit_bytes=24 * 2**20),
        cost_estimate=pl.CostEstimate(
            flops=4 * depth * columns * mine,
            bytes_accessed=2 * depth * (columns + 2 * mine) + 8 * columns * mine,
            transcendentals=0,
        ),
    )(*pieces, *rows)


def place_kernel(spots, order, *refs):
    pieces, out, sems = refs[:len(spots)], refs[-2], refs[-1]
    copies = [
        pltpu.make_async_copy(
            piece, out.at[order[j], pl.ds(row, piece.shape[0])], sems.at[i]
        )
        for i, (piece, (j, row)) in enumerate(zip(pieces, spots))
    ]
    for copy in copies:
        copy.start()
    for copy in copies:
        copy.wait()


def place(order, spots, pieces, rows, into=None):
    columns = pieces[0].shape[1]
    extra = [] if into is None else [into]
    return pl.pallas_call(
        functools.partial(place_kernel, spots),
        out_shape=jax.ShapeDtypeStruct((8, rows, columns), LOW),
        in_specs=[SMEM] + [ANY] * (len(pieces) + len(extra)),
        out_specs=ANY,
        input_output_aliases={1 + len(pieces): 0} if extra else {},
        scratch_shapes=[pltpu.SemaphoreType.DMA((len(pieces),))],
        compiler_params=pltpu.CompilerParams(vmem_limit_bytes=24 * 2**20),
        cost_estimate=pl.CostEstimate(
            flops=0, bytes_accessed=4 * sum(p.size for p in pieces), transcendentals=0
        ),
    )(order, *pieces, *extra)


def add_rows(total, part, start):
    rows = part.shape[0]
    pieces = [total[start:start + rows] + part.astype(F32)]
    if start:
        pieces.insert(0, total[:start])
    if start + rows < total.shape[0]:
        pieces.append(total[start + rows:])
    return jnp.concatenate(pieces, axis=0)


def on_device(tokens, up_out, up_tangent, cotangent, cot_tangent, gate_weight, gate_direction):
    xl, y, c, z, xh = (lax.axis_index(name) for name in AXES)
    depth, wide = gate_weight.shape
    mine = tokens.shape[0]
    half = depth // 2
    same = c == xh
    sign = 1 - 2 * c

    room = -(-wide // 128) * 128
    gap = ((0, 0), (0, room - wide))
    own = jnp.concatenate([jnp.pad(gate_weight, gap), jnp.pad(gate_direction, gap)], axis=1)

    own, turned = after(own, tokens.T)
    near = lax.ppermute(turned, ("c", "xh"), [(2, 0), (1, 3), (0, 1), (3, 2)])
    cross = lax.ppermute(turned, ("c", "xh"), [(2, 1), (1, 2)])
    block = jnp.concatenate([jnp.where(same, turned, near), jnp.where(same, near, cross)], axis=1)

    one = step(own, "y", 1)
    over = swap(own, "xl")
    later, block = after(own, block)
    two = step(later, "y", -1)
    a1, b1 = step(block, "z", 1), step(block, "z", -1)
    one, a1, b1 = after(one, a1, b1)
    a2, b2 = step(a1, "z", 1), step(b1, "z", -1)
    far_one = step(one[:half], "y", 1)
    a3, b3 = step(a2, "z", 1), step(b2, "z", -1)
    far_two = step(two[half:], "y", -1)
    a4, b4 = step(a3[:half], "z", 1), step(b3[half:], "z", -1)
    over, far_one = after(over, far_one)
    over_far_one = swap(far_one, "xl")
    over_one = step(over, "y", 1)
    over, far_two = after(over, far_two)
    over_far_two = swap(far_two, "xl")
    over_two = step(over, "y", -1)
    opposite = jnp.concatenate([a4, b4], axis=0)
    token_blocks = jnp.stack([block, b1, b2, b3, opposite, a3, a2, a1])

    index = jnp.stack([
        (sign * (jnp.bitwise_xor(xl, j // 4) * 4 + (y + sign * j + 8) % 4 - z) + 16) % 8
        for j in range(8)
    ])
    rows_of = [
        lax.dynamic_index_in_dim(token_blocks, index[j], 0, keepdims=False) for j in range(8)
    ]
    early = [(own, 0, 0), (over, 4, 0), (one, 3, 0), (two, 1, 0), (far_one, 2, 0), (far_two, 2, half)]
    late = [(over_far_one, 6, 0), (over_one, 7, 0), (over_far_two, 6, half), (over_two, 5, 0)]
    spots, pieces = [g[1:] for g in early], [g[0] for g in early]
    along = place(index, spots, pieces, depth)
    kept, away = gate_products(
        pieces, [rows_of[j][row:row + piece.shape[0]] for piece, j, row in early]
    )
    along, kept = after(along, kept)
    for piece, j, row in late:
        rows = rows_of[j][row:row + piece.shape[0]]
        kept, away, piece, rows = after(kept, away, piece, rows)
        away = away + dot(piece, rows[:, mine:], ((0,), (0,)))
        if j != 5:
            kept = kept + dot(piece, rows[:, :mine], ((0,), (0,)))
    got = swap(away.astype(LOW), "c")
    kept = kept + dot(piece, rows[:, :mine], ((0,), (0,)))
    spots, pieces = [g[1:] for g in late], [g[0] for g in late]
    along = place(index, spots, pieces, depth, along)
    got, along = after(got, along)

    mixed = backward(kept, got, up_out.T, up_tangent.T, cotangent.T, cot_tangent.T)
    other = swap(mixed, "c")

    everyone = jnp.concatenate([mixed, other], axis=1)

    def tangent(offset):
        return dot(along[offset % 8], everyone, ((1,), (0,)))

    opposite = tangent(4).astype(LOW)
    chain_a = step(opposite[:half], "z", 1)
    chain_b = step(opposite[half:], "z", -1)
    sum_a = add_rows(tangent(3), chain_a, 0).astype(LOW)
    chain_a = step(sum_a, "z", 1)
    sum_b = add_rows(tangent(-3), chain_b, half).astype(LOW)
    back_dot, sum_b = after(everyone[:wide], sum_b)
    chain_b = step(sum_b, "z", -1)

    def curv(other, offset):
        return dot(rows_of[other * 4 + offset], back_dot, ((1,), (1,)))

    got_x = swap(curv(1, 2).astype(LOW), "xl")
    got_one = step(curv(1, 1).astype(LOW), "y", 1)
    got_two = step(curv(1, 3).astype(LOW), "y", -1)
    chain_a = step((tangent(2) + chain_a.astype(F32)).astype(LOW), "z", 1)
    chain_b = step((tangent(-2) + chain_b.astype(F32)).astype(LOW), "z", -1)

    far_sum = (curv(0, 2) + got_x.astype(F32)).astype(LOW)
    far_one = step(far_sum[:half], "y", 1)
    far_two = step(far_sum[half:], "y", -1)
    chain_a = step((tangent(1) + chain_a.astype(F32)).astype(LOW), "z", 1)
    chain_b = step((tangent(-1) + chain_b.astype(F32)).astype(LOW), "z", -1)

    over_sum = (curv(1, 0) + got_one.astype(F32) + got_two.astype(F32)).astype(LOW)
    last_x = swap(over_sum, "xl")
    last_one = step(add_rows(curv(0, 1), far_one, 0).astype(LOW), "y", 1)
    last_two = step(add_rows(curv(0, 3), far_two, half).astype(LOW), "y", -1)
    total = tangent(0) + chain_a.astype(F32) + chain_b.astype(F32)
    of_own, of_other = total[:, :mine], total[:, mine:]
    sent = jnp.where(same, of_other, of_own).astype(LOW)
    near = lax.ppermute(sent, ("c", "xh"), [(1, 0), (2, 3), (0, 2), (3, 1)])
    cross = lax.ppermute(of_other.astype(LOW), ("c", "xh"), [(1, 2), (2, 1)])
    rest = jnp.where(same, of_own, cross.astype(F32))
    input_tangent = (rest + near.astype(F32)).astype(LOW).T

    curvature = (
        curv(0, 0) + last_x.astype(F32) + last_one.astype(F32) + last_two.astype(F32)
    ).astype(LOW)
    return (curvature, input_tangent)


def solution(mesh):
    fine = Mesh(mesh.devices.reshape([SIZES[name] for name in AXES]), AXES)
    spec = P(("xl", "y", "c"), ("z", "xh"))
    return jax.shard_map(
        on_device, mesh=fine, in_specs=(spec,) * 7, out_specs=(spec, spec), check_vma=False
    )
```

```python
import functools

import jax
import jax.numpy as jnp
from jax import lax
from jax.experimental import pallas as pl
from jax.experimental.pallas import tpu as pltpu
from jax.sharding import Mesh, PartitionSpec as P

F32 = jnp.float32
LOW = jnp.bfloat16
SIZES = {"xl": 2, "y": 4, "c": 2, "z": 8, "xh": 2}
AXES = ("xl", "y", "c", "z", "xh")
VMEM = pl.BlockSpec(memory_space=pltpu.VMEM)
SMEM = pl.BlockSpec(memory_space=pltpu.SMEM)
ANY = pl.BlockSpec(memory_space=pl.ANY)


def swap(x, axis):
    return lax.ppermute(x, axis, [(0, 1), (1, 0)])


def step(x, axis, by):
    n = SIZES[axis]
    moves = [(c, i, (i + (by if c == 0 else -by)) % n) for c in range(2) for i in range(n)]
    if axis == "y":
        return lax.ppermute(x, ("y", "c"), [(2 * i + c, 2 * j + c) for c, i, j in moves])
    return lax.ppermute(x, ("c", "z"), [(n * c + i, n * c + j) for c, i, j in moves])


def after(*arrays):
    return lax.optimization_barrier(arrays)


def dot(left, right, dims):
    return lax.dot_general(left, right, (dims, ((), ())), preferred_element_type=F32)


def backward_kernel(kept, got, up_out, up_tangent, cotangent, cot_tangent, out):
    wide, room = up_out.shape[0], kept.shape[0] // 2
    rows = next(n for n in (96, 32, 16) if wide % n == 0)

    def body(i, carry):
        at = pl.ds(pl.multiple_of(i * rows, rows), rows)
        there = pl.ds(pl.multiple_of(i * rows + room, 16), rows)
        gate = kept[at, :] + got[at, :].astype(F32)
        gate_dot = kept[there, :] + got[there, :].astype(F32)
        sig = 1.0 / (1.0 + jnp.exp(-gate))
        first = sig * (1.0 + gate * (1.0 - sig))
        second = sig * (1.0 - sig) * (2.0 + gate * (1.0 - 2.0 * sig))
        up_val = up_out[at, :].astype(F32)
        cot_val = cotangent[at, :].astype(F32)
        up_dir = up_tangent[at, :].astype(F32)
        cot_dir = cot_tangent[at, :].astype(F32)
        both = cot_val * up_val
        out[there, :] = (both * first).astype(LOW)
        out[at, :] = (
            cot_dir * up_val * first + cot_val * up_dir * first + both * second * gate_dot
        ).astype(LOW)
        return carry

    lax.fori_loop(0, wide // rows, body, 0)
    if room > wide:
        gap = jnp.zeros((room - wide, out.shape[1]), LOW)
        out[wide:room, :] = gap
        out[room + wide:, :] = gap


def backward(kept, got, up_out, up_tangent, cotangent, cot_tangent):
    return pl.pallas_call(
        backward_kernel,
        out_shape=jax.ShapeDtypeStruct(kept.shape, LOW),
        in_specs=[VMEM] * 6,
        out_specs=VMEM,
        compiler_params=pltpu.CompilerParams(vmem_limit_bytes=24 * 2**20),
        cost_estimate=pl.CostEstimate(
            flops=20 * kept.size, bytes_accessed=14 * kept.size, transcendentals=kept.size // 2
        ),
    )(kept, got, up_out, up_tangent, cotangent, cot_tangent)


def gate_kernel(count, *refs):
    pieces, rows, kept, away = refs[:count], refs[count:-2], refs[-2], refs[-1]
    mine = kept.shape[1]
    tile = next(n for n in (256, 128, 64) if kept.shape[0] % n == 0)

    def body(i, carry):
        at = pl.ds(pl.multiple_of(i * tile, tile), tile)
        total = None
        for piece, row in zip(pieces, rows):
            part = dot(piece[:, at], row[...], ((0,), (0,)))
            total = part if total is None else total + part
        kept[at, :] = total[:, :mine]
        away[at, :] = total[:, mine:]
        return carry

    lax.fori_loop(0, kept.shape[0] // tile, body, 0)


def gate_products(pieces, rows):
    columns, mine = pieces[0].shape[1], rows[0].shape[1] // 2
    depth = sum(p.shape[0] for p in pieces)
    return pl.pallas_call(
        functools.partial(gate_kernel, len(pieces)),
        out_shape=(jax.ShapeDtypeStruct((columns, mine), F32),) * 2,
        in_specs=[VMEM] * (2 * len(pieces)),
        out_specs=(VMEM, VMEM),
        compiler_params=pltpu.CompilerParams(vmem_limit_bytes=24 * 2**20),
        cost_estimate=pl.CostEstimate(
            flops=4 * depth * columns * mine,
            bytes_accessed=2 * depth * (columns + 2 * mine) + 8 * columns * mine,
            transcendentals=0,
        ),
    )(*pieces, *rows)


def place_kernel(numbers, order, *refs):
    blocks, out, sems = refs[:len(numbers)], refs[-2], refs[-1]
    copies = [
        pltpu.make_async_copy(block, out.at[order[j]], sems.at[i])
        for i, (block, j) in enumerate(zip(blocks, numbers))
    ]
    for copy in copies:
        copy.start()
    for copy in copies:
        copy.wait()


def place(order, numbers, blocks, into=None):
    shape, count = blocks[0].shape, len(blocks)
    extra = [] if into is None else [into]
    return pl.pallas_call(
        functools.partial(place_kernel, numbers),
        out_shape=jax.ShapeDtypeStruct((8,) + shape, LOW),
        in_specs=[SMEM] + [ANY] * (count + len(extra)),
        out_specs=ANY,
        input_output_aliases={1 + count: 0} if extra else {},
        scratch_shapes=[pltpu.SemaphoreType.DMA((count,))],
        compiler_params=pltpu.CompilerParams(vmem_limit_bytes=24 * 2**20),
        cost_estimate=pl.CostEstimate(
            flops=0, bytes_accessed=4 * count * shape[0] * shape[1], transcendentals=0
        ),
    )(order, *blocks, *extra)


def on_device(tokens, up_out, up_tangent, cotangent, cot_tangent, gate_weight, gate_direction):
    xl, y, c, z, xh = (lax.axis_index(name) for name in AXES)
    wide = gate_weight.shape[1]
    mine = tokens.shape[0]
    same = c == xh
    sign = 1 - 2 * c

    room = -(-wide // 128) * 128
    gap = ((0, 0), (0, room - wide))
    own = jnp.concatenate([jnp.pad(gate_weight, gap), jnp.pad(gate_direction, gap)], axis=1)

    own, turned = after(own, tokens.T)
    near = lax.ppermute(turned, ("c", "xh"), [(2, 0), (1, 3), (0, 1), (3, 2)])
    cross = lax.ppermute(turned, ("c", "xh"), [(2, 1), (1, 2)])
    block = jnp.concatenate([jnp.where(same, turned, near), jnp.where(same, near, cross)], axis=1)

    one = step(own, "y", 1)
    over = swap(own, "xl")
    later, block = after(own, block)
    two = step(later, "y", -1)
    a1, b1 = step(block, "z", 1), step(block, "z", -1)
    one, a1, b1 = after(one, a1, b1)
    a2, b2 = step(a1, "z", 1), step(b1, "z", -1)
    far = step(one, "y", 1)
    two, over, a2, b2 = after(two, over, a2, b2)
    a3, b3 = step(a2, "z", 1), step(b2, "z", -1)
    over, far, a3 = after(over, far, a3)
    over_far = swap(far, "xl")
    over_one = step(over, "y", 1)
    over_two = step(over, "y", -1)
    a4 = step(a3, "z", 1)
    token_blocks = jnp.stack([block, b1, b2, b3, a4, a3, a2, a1])

    index = jnp.stack([
        (sign * (jnp.bitwise_xor(xl, j // 4) * 4 + (y + sign * j + 8) % 4 - z) + 16) % 8
        for j in range(8)
    ])
    rows_of = [
        lax.dynamic_index_in_dim(token_blocks, index[j], 0, keepdims=False) for j in range(8)
    ]
    early, late = {0: own, 4: over, 3: one, 1: two, 2: far}, {6: over_far, 7: over_one, 5: over_two}
    along = place(index, list(early), list(early.values()))
    kept, away = gate_products(list(early.values()), [rows_of[j] for j in early])
    along, kept = after(along, kept)
    for j, piece in late.items():
        kept, away, piece, rows = after(kept, away, piece, rows_of[j])
        away = away + dot(piece, rows[:, mine:], ((0,), (0,)))
        if j != 5:
            kept = kept + dot(piece, rows[:, :mine], ((0,), (0,)))
    got = swap(away.astype(LOW), "c")
    kept = kept + dot(piece, rows[:, :mine], ((0,), (0,)))
    along = place(index, list(late), list(late.values()), along)
    got, along = after(got, along)

    mixed = backward(kept, got, up_out.T, up_tangent.T, cotangent.T, cot_tangent.T)
    other = swap(mixed, "c")

    everyone = jnp.concatenate([mixed, other], axis=1)

    def tangent(offset):
        return dot(along[offset % 8], everyone, ((1,), (0,)))

    chain_a = step(tangent(4).astype(LOW), "z", 1)
    chain_b = step(tangent(-3).astype(LOW), "z", -1)
    sum_a = (tangent(3) + chain_a.astype(F32)).astype(LOW)
    back_dot, sum_a = after(everyone[:wide], sum_a)
    chain_a = step(sum_a, "z", 1)

    def curv(other, offset):
        return dot(rows_of[other * 4 + offset], back_dot, ((1,), (1,)))

    got_x = swap(curv(1, 2).astype(LOW), "xl")
    got_one = step(curv(1, 1).astype(LOW), "y", 1)
    got_two = step(curv(1, 3).astype(LOW), "y", -1)
    chain_b = step((tangent(-2) + chain_b.astype(F32)).astype(LOW), "z", -1)
    chain_a = step((tangent(2) + chain_a.astype(F32)).astype(LOW), "z", 1)
    sum_b = (tangent(-1) + chain_b.astype(F32)).astype(LOW)
    got_x, got_one, got_two, sum_b = after(got_x, got_one, got_two, sum_b)
    far = step((curv(0, 2) + got_x.astype(F32)).astype(LOW), "y", 1)
    chain_b = step(sum_b, "z", -1)
    chain_a = step((tangent(1) + chain_a.astype(F32)).astype(LOW), "z", 1)
    over_sum = (curv(1, 0) + got_one.astype(F32) + got_two.astype(F32)).astype(LOW)
    last_x = swap(over_sum, "xl")
    last_two = step(curv(0, 3).astype(LOW), "y", -1)
    last_one = step((curv(0, 1) + far.astype(F32)).astype(LOW), "y", 1)
    total = tangent(0) + chain_a.astype(F32) + chain_b.astype(F32)
    of_own, of_other = total[:, :mine], total[:, mine:]
    sent = jnp.where(same, of_other, of_own).astype(LOW)
    near = lax.ppermute(sent, ("c", "xh"), [(1, 0), (2, 3), (0, 2), (3, 1)])
    cross = lax.ppermute(of_other.astype(LOW), ("c", "xh"), [(1, 2), (2, 1)])
    rest = jnp.where(same, of_own, cross.astype(F32))
    input_tangent = (rest + near.astype(F32)).astype(LOW).T

    curvature = (
        curv(0, 0) + last_x.astype(F32) + last_one.astype(F32) + last_two.astype(F32)
    ).astype(LOW)
    return (curvature, input_tangent)


def solution(mesh):
    fine = Mesh(mesh.devices.reshape([SIZES[name] for name in AXES]), AXES)
    spec = P(("xl", "y", "c"), ("z", "xh"))
    return jax.shard_map(
        on_device, mesh=fine, in_specs=(spec,) * 7, out_specs=(spec, spec), check_vma=False
    )
```

```python
import functools

import jax
import jax.numpy as jnp
from jax import lax
from jax.experimental import pallas as pl
from jax.experimental.pallas import tpu as pltpu
from jax.sharding import Mesh, PartitionSpec as P

F32 = jnp.float32
LOW = jnp.bfloat16
SIZES = {"xl": 2, "y": 4, "c": 2, "z": 8, "xh": 2}
AXES = ("xl", "y", "c", "z", "xh")
VMEM = pl.BlockSpec(memory_space=pltpu.VMEM)
SMEM = pl.BlockSpec(memory_space=pltpu.SMEM)
ANY = pl.BlockSpec(memory_space=pl.ANY)


def swap(x, axis):
    return lax.ppermute(x, axis, [(0, 1), (1, 0)])


def step(x, axis, by):
    n = SIZES[axis]
    moves = [(c, i, (i + (by if c == 0 else -by)) % n) for c in range(2) for i in range(n)]
    if axis == "y":
        return lax.ppermute(x, ("y", "c"), [(2 * i + c, 2 * j + c) for c, i, j in moves])
    return lax.ppermute(x, ("c", "z"), [(n * c + i, n * c + j) for c, i, j in moves])


def after(*arrays):
    return lax.optimization_barrier(arrays)


def dot(left, right, dims):
    return lax.dot_general(left, right, (dims, ((), ())), preferred_element_type=F32)


def backward_kernel(kept, got, up_out, up_tangent, cotangent, cot_tangent, out):
    wide, room = up_out.shape[0], kept.shape[0] // 2
    rows = next(n for n in (96, 32, 16) if wide % n == 0)

    def body(i, carry):
        at = pl.ds(pl.multiple_of(i * rows, rows), rows)
        there = pl.ds(pl.multiple_of(i * rows + room, 16), rows)
        gate = kept[at, :] + got[at, :].astype(F32)
        gate_dot = kept[there, :] + got[there, :].astype(F32)
        sig = 1.0 / (1.0 + jnp.exp(-gate))
        first = sig * (1.0 + gate * (1.0 - sig))
        second = sig * (1.0 - sig) * (2.0 + gate * (1.0 - 2.0 * sig))
        up_val = up_out[at, :].astype(F32)
        cot_val = cotangent[at, :].astype(F32)
        up_dir = up_tangent[at, :].astype(F32)
        cot_dir = cot_tangent[at, :].astype(F32)
        both = cot_val * up_val
        out[there, :] = (both * first).astype(LOW)
        out[at, :] = (
            cot_dir * up_val * first + cot_val * up_dir * first + both * second * gate_dot
        ).astype(LOW)
        return carry

    lax.fori_loop(0, wide // rows, body, 0)
    if room > wide:
        gap = jnp.zeros((room - wide, out.shape[1]), LOW)
        out[wide:room, :] = gap
        out[room + wide:, :] = gap


def backward(kept, got, up_out, up_tangent, cotangent, cot_tangent):
    return pl.pallas_call(
        backward_kernel,
        out_shape=jax.ShapeDtypeStruct(kept.shape, LOW),
        in_specs=[VMEM] * 6,
        out_specs=VMEM,
        compiler_params=pltpu.CompilerParams(vmem_limit_bytes=24 * 2**20),
        cost_estimate=pl.CostEstimate(
            flops=20 * kept.size, bytes_accessed=14 * kept.size, transcendentals=kept.size // 2
        ),
    )(kept, got, up_out, up_tangent, cotangent, cot_tangent)


def gate_kernel(count, *refs):
    pieces, rows, kept, away = refs[:count], refs[count:-2], refs[-2], refs[-1]
    mine = kept.shape[1]
    tile = next(n for n in (256, 128, 64) if kept.shape[0] % n == 0)

    def body(i, carry):
        at = pl.ds(pl.multiple_of(i * tile, tile), tile)
        total = None
        for piece, row in zip(pieces, rows):
            part = dot(piece[:, at], row[...], ((0,), (0,)))
            total = part if total is None else total + part
        kept[at, :] = total[:, :mine]
        away[at, :] = total[:, mine:]
        return carry

    lax.fori_loop(0, kept.shape[0] // tile, body, 0)


def gate_products(pieces, rows):
    columns, mine = pieces[0].shape[1], rows[0].shape[1] // 2
    depth = sum(p.shape[0] for p in pieces)
    return pl.pallas_call(
        functools.partial(gate_kernel, len(pieces)),
        out_shape=(jax.ShapeDtypeStruct((columns, mine), F32),) * 2,
        in_specs=[VMEM] * (2 * len(pieces)),
        out_specs=(VMEM, VMEM),
        compiler_params=pltpu.CompilerParams(vmem_limit_bytes=24 * 2**20),
        cost_estimate=pl.CostEstimate(
            flops=4 * depth * columns * mine,
            bytes_accessed=2 * depth * (columns + 2 * mine) + 8 * columns * mine,
            transcendentals=0,
        ),
    )(*pieces, *rows)


def place_kernel(spots, order, *refs):
    pieces, out, sems = refs[:len(spots)], refs[-2], refs[-1]
    copies = [
        pltpu.make_async_copy(
            piece, out.at[order[j], pl.ds(row, piece.shape[0])], sems.at[i]
        )
        for i, (piece, (j, row)) in enumerate(zip(pieces, spots))
    ]
    for copy in copies:
        copy.start()
    for copy in copies:
        copy.wait()


def place(order, spots, pieces, rows, into=None):
    columns = pieces[0].shape[1]
    extra = [] if into is None else [into]
    return pl.pallas_call(
        functools.partial(place_kernel, spots),
        out_shape=jax.ShapeDtypeStruct((8, rows, columns), LOW),
        in_specs=[SMEM] + [ANY] * (len(pieces) + len(extra)),
        out_specs=ANY,
        input_output_aliases={1 + len(pieces): 0} if extra else {},
        scratch_shapes=[pltpu.SemaphoreType.DMA((len(pieces),))],
        compiler_params=pltpu.CompilerParams(vmem_limit_bytes=24 * 2**20),
        cost_estimate=pl.CostEstimate(
            flops=0, bytes_accessed=4 * sum(p.size for p in pieces), transcendentals=0
        ),
    )(order, *pieces, *extra)


def on_device(tokens, up_out, up_tangent, cotangent, cot_tangent, gate_weight, gate_direction):
    xl, y, c, z, xh = (lax.axis_index(name) for name in AXES)
    depth, wide = gate_weight.shape
    mine = tokens.shape[0]
    half = depth // 2
    same = c == xh
    sign = 1 - 2 * c

    room = -(-wide // 128) * 128
    gap = ((0, 0), (0, room - wide))
    own = jnp.concatenate([jnp.pad(gate_weight, gap), jnp.pad(gate_direction, gap)], axis=1)

    own, turned = after(own, tokens.T)
    near = lax.ppermute(turned, ("c", "xh"), [(2, 0), (1, 3), (0, 1), (3, 2)])
    cross = lax.ppermute(turned, ("c", "xh"), [(2, 1), (1, 2)])
    block = jnp.concatenate([jnp.where(same, turned, near), jnp.where(same, near, cross)], axis=1)

    one = step(own, "y", 1)
    over = swap(own, "xl")
    later, block = after(own, block)
    two = step(later, "y", -1)
    a1, b1 = step(block, "z", 1), step(block, "z", -1)
    one, a1, b1 = after(one, a1, b1)
    a2, b2 = step(a1, "z", 1), step(b1, "z", -1)
    far_one = step(one[:half], "y", 1)
    a3, b3 = step(a2, "z", 1), step(b2, "z", -1)
    far_two = step(two[half:], "y", -1)
    a4, b4 = step(a3[:half], "z", 1), step(b3[half:], "z", -1)
    over, far_one = after(over, far_one)
    over_far_one = swap(far_one, "xl")
    over_one = step(over, "y", 1)
    over, far_two = after(over, far_two)
    over_far_two = swap(far_two, "xl")
    over_two = step(over, "y", -1)
    opposite = jnp.concatenate([a4, b4], axis=0)
    token_blocks = jnp.stack([block, b1, b2, b3, opposite, a3, a2, a1])

    index = jnp.stack([
        (sign * (jnp.bitwise_xor(xl, j // 4) * 4 + (y + sign * j + 8) % 4 - z) + 16) % 8
        for j in range(8)
    ])
    rows_of = [
        lax.dynamic_index_in_dim(token_blocks, index[j], 0, keepdims=False) for j in range(8)
    ]
    early = [(own, 0, 0), (over, 4, 0), (one, 3, 0), (two, 1, 0), (far_one, 2, 0), (far_two, 2, half)]
    late = [(over_far_one, 6, 0), (over_one, 7, 0), (over_far_two, 6, half), (over_two, 5, 0)]
    spots, pieces = [g[1:] for g in early], [g[0] for g in early]
    along = place(index, spots, pieces, depth)
    kept, away = gate_products(
        pieces, [rows_of[j][row:row + piece.shape[0]] for piece, j, row in early]
    )
    along, kept = after(along, kept)
    for piece, j, row in late:
        rows = rows_of[j][row:row + piece.shape[0]]
        kept, away, piece, rows = after(kept, away, piece, rows)
        away = away + dot(piece, rows[:, mine:], ((0,), (0,)))
        if j != 5:
            kept = kept + dot(piece, rows[:, :mine], ((0,), (0,)))
    got = swap(away.astype(LOW), "c")
    kept = kept + dot(piece, rows[:, :mine], ((0,), (0,)))
    spots, pieces = [g[1:] for g in late], [g[0] for g in late]
    along = place(index, spots, pieces, depth, along)
    got, along = after(got, along)

    mixed = backward(kept, got, up_out.T, up_tangent.T, cotangent.T, cot_tangent.T)
    other = swap(mixed, "c")

    everyone = jnp.concatenate([mixed, other], axis=1)

    def tangent(offset):
        return dot(along[offset % 8], everyone, ((1,), (0,)))

    chain_a = step(tangent(4).astype(LOW), "z", 1)
    chain_b = step(tangent(-3).astype(LOW), "z", -1)
    sum_a = (tangent(3) + chain_a.astype(F32)).astype(LOW)
    back_dot, sum_a = after(everyone[:wide], sum_a)
    chain_a = step(sum_a, "z", 1)

    def curv(other, offset):
        return dot(rows_of[other * 4 + offset], back_dot, ((1,), (1,)))

    got_x = swap(curv(1, 2).astype(LOW), "xl")
    got_one = step(curv(1, 1).astype(LOW), "y", 1)
    got_two = step(curv(1, 3).astype(LOW), "y", -1)
    second_a, second_b, sum_b = after(tangent(2), tangent(-2), chain_b)
    chain_b = step((second_b + sum_b.astype(F32)).astype(LOW), "z", -1)
    first_a, first_b, at_home, sum_a = after(tangent(1), tangent(-1), tangent(0), chain_a)
    chain_a = step((second_a + sum_a.astype(F32)).astype(LOW), "z", 1)
    sum_b = (first_b + chain_b.astype(F32)).astype(LOW)
    got_x, sum_b = after(got_x, sum_b)
    far = step((curv(0, 2) + got_x.astype(F32)).astype(LOW), "y", 1)
    chain_b = step(sum_b, "z", -1)
    chain_a = step((first_a + chain_a.astype(F32)).astype(LOW), "z", 1)
    over_sum = (curv(1, 0) + got_one.astype(F32) + got_two.astype(F32)).astype(LOW)
    last_x = swap(over_sum, "xl")
    last_two = step(curv(0, 3).astype(LOW), "y", -1)
    last_one = step((curv(0, 1) + far.astype(F32)).astype(LOW), "y", 1)
    total = at_home + chain_a.astype(F32) + chain_b.astype(F32)
    of_own, of_other = total[:, :mine], total[:, mine:]
    sent = jnp.where(same, of_other, of_own).astype(LOW)
    near = lax.ppermute(sent, ("c", "xh"), [(1, 0), (2, 3), (0, 2), (3, 1)])
    cross = lax.ppermute(of_other.astype(LOW), ("c", "xh"), [(1, 2), (2, 1)])
    rest = jnp.where(same, of_own, cross.astype(F32))
    input_tangent = (rest + near.astype(F32)).astype(LOW).T

    curvature = (
        curv(0, 0) + last_x.astype(F32) + last_one.astype(F32) + last_two.astype(F32)
    ).astype(LOW)
    return (curvature, input_tangent)


def solution(mesh):
    fine = Mesh(mesh.devices.reshape([SIZES[name] for name in AXES]), AXES)
    spec = P(("xl", "y", "c"), ("z", "xh"))
    return jax.shard_map(
        on_device, mesh=fine, in_specs=(spec,) * 7, out_specs=(spec, spec), check_vma=False
    )
```

```python
import functools

import jax
import jax.numpy as jnp
from jax import lax
from jax.experimental import pallas as pl
from jax.experimental.pallas import tpu as pltpu
from jax.sharding import Mesh, PartitionSpec as P

F32 = jnp.float32
LOW = jnp.bfloat16
SIZES = {"xl": 2, "y": 4, "c": 2, "z": 8, "xh": 2}
AXES = ("xl", "y", "c", "z", "xh")
VMEM = pl.BlockSpec(memory_space=pltpu.VMEM)
SMEM = pl.BlockSpec(memory_space=pltpu.SMEM)
ANY = pl.BlockSpec(memory_space=pl.ANY)


def swap(x, axis):
    return lax.ppermute(x, axis, [(0, 1), (1, 0)])


def step(x, axis, by):
    n = SIZES[axis]
    moves = [(c, i, (i + (by if c == 0 else -by)) % n) for c in range(2) for i in range(n)]
    if axis == "y":
        return lax.ppermute(x, ("y", "c"), [(2 * i + c, 2 * j + c) for c, i, j in moves])
    return lax.ppermute(x, ("c", "z"), [(n * c + i, n * c + j) for c, i, j in moves])


def after(*arrays):
    return lax.optimization_barrier(arrays)


def dot(left, right, dims):
    return lax.dot_general(left, right, (dims, ((), ())), preferred_element_type=F32)


def backward_kernel(kept, got, up_out, up_tangent, cotangent, cot_tangent, out):
    wide, room = up_out.shape[0], kept.shape[0] // 2
    rows = next(n for n in (96, 32, 16) if wide % n == 0)

    def body(i, carry):
        at = pl.ds(pl.multiple_of(i * rows, rows), rows)
        there = pl.ds(pl.multiple_of(i * rows + room, 16), rows)
        gate = kept[at, :] + got[at, :].astype(F32)
        gate_dot = kept[there, :] + got[there, :].astype(F32)
        sig = 1.0 / (1.0 + jnp.exp(-gate))
        first = sig * (1.0 + gate * (1.0 - sig))
        second = sig * (1.0 - sig) * (2.0 + gate * (1.0 - 2.0 * sig))
        up_val = up_out[at, :].astype(F32)
        cot_val = cotangent[at, :].astype(F32)
        up_dir = up_tangent[at, :].astype(F32)
        cot_dir = cot_tangent[at, :].astype(F32)
        both = cot_val * up_val
        out[there, :] = (both * first).astype(LOW)
        out[at, :] = (
            cot_dir * up_val * first + cot_val * up_dir * first + both * second * gate_dot
        ).astype(LOW)
        return carry

    lax.fori_loop(0, wide // rows, body, 0)
    if room > wide:
        gap = jnp.zeros((room - wide, out.shape[1]), LOW)
        out[wide:room, :] = gap
        out[room + wide:, :] = gap


def backward(kept, got, up_out, up_tangent, cotangent, cot_tangent):
    return pl.pallas_call(
        backward_kernel,
        out_shape=jax.ShapeDtypeStruct(kept.shape, LOW),
        in_specs=[VMEM] * 6,
        out_specs=VMEM,
        compiler_params=pltpu.CompilerParams(vmem_limit_bytes=24 * 2**20),
        cost_estimate=pl.CostEstimate(
            flops=20 * kept.size, bytes_accessed=14 * kept.size, transcendentals=kept.size // 2
        ),
    )(kept, got, up_out, up_tangent, cotangent, cot_tangent)


def gate_kernel(count, *refs):
    pieces, rows, kept, away = refs[:count], refs[count:-2], refs[-2], refs[-1]
    mine = kept.shape[1]
    tile = next(n for n in (256, 128, 64) if kept.shape[0] % n == 0)

    def body(i, carry):
        at = pl.ds(pl.multiple_of(i * tile, tile), tile)
        total = None
        for piece, row in zip(pieces, rows):
            part = dot(piece[:, at], row[...], ((0,), (0,)))
            total = part if total is None else total + part
        kept[at, :] = total[:, :mine]
        away[at, :] = total[:, mine:]
        return carry

    lax.fori_loop(0, kept.shape[0] // tile, body, 0)


def gate_products(pieces, rows):
    columns, mine = pieces[0].shape[1], rows[0].shape[1] // 2
    depth = sum(p.shape[0] for p in pieces)
    return pl.pallas_call(
        functools.partial(gate_kernel, len(pieces)),
        out_shape=(jax.ShapeDtypeStruct((columns, mine), F32),) * 2,
        in_specs=[VMEM] * (2 * len(pieces)),
        out_specs=(VMEM, VMEM),
        compiler_params=pltpu.CompilerParams(vmem_limit_bytes=24 * 2**20),
        cost_estimate=pl.CostEstimate(
            flops=4 * depth * columns * mine,
            bytes_accessed=2 * depth * (columns + 2 * mine) + 8 * columns * mine,
            transcendentals=0,
        ),
    )(*pieces, *rows)


def place_kernel(spots, order, *refs):
    pieces, out, sems = refs[:len(spots)], refs[-2], refs[-1]
    copies = [
        pltpu.make_async_copy(
            piece, out.at[order[j], pl.ds(row, piece.shape[0])], sems.at[i]
        )
        for i, (piece, (j, row)) in enumerate(zip(pieces, spots))
    ]
    for copy in copies:
        copy.start()
    for copy in copies:
        copy.wait()


def place(order, spots, pieces, rows, into=None):
    columns = pieces[0].shape[1]
    extra = [] if into is None else [into]
    return pl.pallas_call(
        functools.partial(place_kernel, spots),
        out_shape=jax.ShapeDtypeStruct((8, rows, columns), LOW),
        in_specs=[SMEM] + [ANY] * (len(pieces) + len(extra)),
        out_specs=ANY,
        input_output_aliases={1 + len(pieces): 0} if extra else {},
        scratch_shapes=[pltpu.SemaphoreType.DMA((len(pieces),))],
        compiler_params=pltpu.CompilerParams(vmem_limit_bytes=24 * 2**20),
        cost_estimate=pl.CostEstimate(
            flops=0, bytes_accessed=4 * sum(p.size for p in pieces), transcendentals=0
        ),
    )(order, *pieces, *extra)


def add_rows(total, part, start):
    rows = part.shape[0]
    pieces = [total[start:start + rows] + part.astype(F32)]
    if start:
        pieces.insert(0, total[:start])
    if start + rows < total.shape[0]:
        pieces.append(total[start + rows:])
    return jnp.concatenate(pieces, axis=0)


def on_device(tokens, up_out, up_tangent, cotangent, cot_tangent, gate_weight, gate_direction):
    xl, y, c, z, xh = (lax.axis_index(name) for name in AXES)
    depth, wide = gate_weight.shape
    mine = tokens.shape[0]
    half = depth // 2
    same = c == xh
    sign = 1 - 2 * c

    room = -(-wide // 128) * 128
    gap = ((0, 0), (0, room - wide))
    own = jnp.concatenate([jnp.pad(gate_weight, gap), jnp.pad(gate_direction, gap)], axis=1)

    own, turned = after(own, tokens.T)
    near = lax.ppermute(turned, ("c", "xh"), [(2, 0), (1, 3), (0, 1), (3, 2)])
    cross = lax.ppermute(turned, ("c", "xh"), [(2, 1), (1, 2)])
    block = jnp.concatenate([jnp.where(same, turned, near), jnp.where(same, near, cross)], axis=1)

    one = step(own, "y", 1)
    over = swap(own, "xl")
    later, block = after(own, block)
    two = step(later, "y", -1)
    a1, b1 = step(block, "z", 1), step(block, "z", -1)
    one, a1, b1 = after(one, a1, b1)
    a2, b2 = step(a1, "z", 1), step(b1, "z", -1)
    far_one = step(one[:half], "y", 1)
    a3, b3 = step(a2, "z", 1), step(b2, "z", -1)
    far_two = step(two[half:], "y", -1)
    a4, b4 = step(a3[:half], "z", 1), step(b3[half:], "z", -1)
    over, far_one = after(over, far_one)
    over_far_one = swap(far_one, "xl")
    over_one = step(over, "y", 1)
    over, far_two = after(over, far_two)
    over_far_two = swap(far_two, "xl")
    over_two = step(over, "y", -1)
    opposite = jnp.concatenate([a4, b4], axis=0)
    token_blocks = jnp.stack([block, b1, b2, b3, opposite, a3, a2, a1])

    index = jnp.stack([
        (sign * (jnp.bitwise_xor(xl, j // 4) * 4 + (y + sign * j + 8) % 4 - z) + 16) % 8
        for j in range(8)
    ])
    rows_of = [
        lax.dynamic_index_in_dim(token_blocks, index[j], 0, keepdims=False) for j in range(8)
    ]
    early = [(own, 0, 0), (over, 4, 0), (one, 3, 0), (two, 1, 0), (far_one, 2, 0), (far_two, 2, half)]
    late = [(over_far_one, 6, 0), (over_one, 7, 0), (over_far_two, 6, half), (over_two, 5, 0)]
    spots, pieces = [g[1:] for g in early], [g[0] for g in early]
    along = place(index, spots, pieces, depth)
    kept, away = gate_products(
        pieces, [rows_of[j][row:row + piece.shape[0]] for piece, j, row in early]
    )
    along, kept = after(along, kept)
    for piece, j, row in late:
        rows = rows_of[j][row:row + piece.shape[0]]
        kept, away, piece, rows = after(kept, away, piece, rows)
        away = away + dot(piece, rows[:, mine:], ((0,), (0,)))
        if j != 5:
            kept = kept + dot(piece, rows[:, :mine], ((0,), (0,)))
    got = swap(away.astype(LOW), "c")
    kept = kept + dot(piece, rows[:, :mine], ((0,), (0,)))
    spots, pieces = [g[1:] for g in late], [g[0] for g in late]
    along = place(index, spots, pieces, depth, along)
    got, along = after(got, along)

    mixed = backward(kept, got, up_out.T, up_tangent.T, cotangent.T, cot_tangent.T)
    other = swap(mixed, "c")

    everyone = jnp.concatenate([mixed, other], axis=1)

    def tangent(offset):
        return dot(along[offset % 8], everyone, ((1,), (0,)))

    chain_a = step(tangent(4).astype(LOW), "z", 1)
    chain_b = step(tangent(-3).astype(LOW), "z", -1)
    sum_a = (tangent(3) + chain_a.astype(F32)).astype(LOW)
    back_dot, sum_a = after(everyone[:wide], sum_a)
    chain_a = step(sum_a, "z", 1)

    def curv(other, offset):
        return dot(rows_of[other * 4 + offset], back_dot, ((1,), (1,)))

    got_x = swap(curv(1, 2).astype(LOW), "xl")
    got_one = step(curv(1, 1).astype(LOW), "y", 1)
    got_two = step(curv(1, 3).astype(LOW), "y", -1)
    second_a, second_b, sum_b = after(tangent(2), tangent(-2), chain_b)
    chain_b = step((second_b + sum_b.astype(F32)).astype(LOW), "z", -1)
    first_a, first_b, at_home, sum_a = after(tangent(1), tangent(-1), tangent(0), chain_a)
    chain_a = step((second_a + sum_a.astype(F32)).astype(LOW), "z", 1)
    far_sum = (curv(0, 2) + got_x.astype(F32)).astype(LOW)
    far_one = step(far_sum[:half], "y", 1)
    far_two = step(far_sum[half:], "y", -1)
    chain_b = step((first_b + chain_b.astype(F32)).astype(LOW), "z", -1)
    chain_a = step((first_a + chain_a.astype(F32)).astype(LOW), "z", 1)
    over_sum = (curv(1, 0) + got_one.astype(F32) + got_two.astype(F32)).astype(LOW)
    last_x = swap(over_sum, "xl")
    last_one = step(add_rows(curv(0, 1), far_one, 0).astype(LOW), "y", 1)
    last_two = step(add_rows(curv(0, 3), far_two, half).astype(LOW), "y", -1)
    total = at_home + chain_a.astype(F32) + chain_b.astype(F32)
    of_own, of_other = total[:, :mine], total[:, mine:]
    sent = jnp.where(same, of_other, of_own).astype(LOW)
    near = lax.ppermute(sent, ("c", "xh"), [(1, 0), (2, 3), (0, 2), (3, 1)])
    cross = lax.ppermute(of_other.astype(LOW), ("c", "xh"), [(1, 2), (2, 1)])
    rest = jnp.where(same, of_own, cross.astype(F32))
    input_tangent = (rest + near.astype(F32)).astype(LOW).T

    curvature = (
        curv(0, 0) + last_x.astype(F32) + last_one.astype(F32) + last_two.astype(F32)
    ).astype(LOW)
    return (curvature, input_tangent)


def solution(mesh):
    fine = Mesh(mesh.devices.reshape([SIZES[name] for name in AXES]), AXES)
    spec = P(("xl", "y", "c"), ("z", "xh"))
    return jax.shard_map(
        on_device, mesh=fine, in_specs=(spec,) * 7, out_specs=(spec, spec), check_vma=False
    )
```

```python
import functools

import jax
import jax.numpy as jnp
from jax import lax
from jax.experimental import pallas as pl
from jax.experimental.pallas import tpu as pltpu
from jax.sharding import Mesh, PartitionSpec as P

F32 = jnp.float32
LOW = jnp.bfloat16
SIZES = {"xl": 2, "y": 4, "c": 2, "z": 8, "xh": 2}
AXES = ("xl", "y", "c", "z", "xh")
VMEM = pl.BlockSpec(memory_space=pltpu.VMEM)
SMEM = pl.BlockSpec(memory_space=pltpu.SMEM)
ANY = pl.BlockSpec(memory_space=pl.ANY)


def swap(x, axis):
    return lax.ppermute(x, axis, [(0, 1), (1, 0)])


def step(x, axis, by):
    n = SIZES[axis]
    moves = [(c, i, (i + (by if c == 0 else -by)) % n) for c in range(2) for i in range(n)]
    if axis == "y":
        return lax.ppermute(x, ("y", "c"), [(2 * i + c, 2 * j + c) for c, i, j in moves])
    return lax.ppermute(x, ("c", "z"), [(n * c + i, n * c + j) for c, i, j in moves])


def after(*arrays):
    return lax.optimization_barrier(arrays)


def dot(left, right, dims):
    return lax.dot_general(left, right, (dims, ((), ())), preferred_element_type=F32)


def backward_kernel(kept, got, up_out, up_tangent, cotangent, cot_tangent, out):
    wide, room = up_out.shape[0], kept.shape[0] // 2
    rows = next(n for n in (96, 32, 16) if wide % n == 0)

    def body(i, carry):
        at = pl.ds(pl.multiple_of(i * rows, rows), rows)
        there = pl.ds(pl.multiple_of(i * rows + room, 16), rows)
        gate = kept[at, :] + got[at, :].astype(F32)
        gate_dot = kept[there, :] + got[there, :].astype(F32)
        sig = 1.0 / (1.0 + jnp.exp(-gate))
        first = sig * (1.0 + gate * (1.0 - sig))
        second = sig * (1.0 - sig) * (2.0 + gate * (1.0 - 2.0 * sig))
        up_val = up_out[at, :].astype(F32)
        cot_val = cotangent[at, :].astype(F32)
        up_dir = up_tangent[at, :].astype(F32)
        cot_dir = cot_tangent[at, :].astype(F32)
        both = cot_val * up_val
        out[there, :] = (both * first).astype(LOW)
        out[at, :] = (
            cot_dir * up_val * first + cot_val * up_dir * first + both * second * gate_dot
        ).astype(LOW)
        return carry

    lax.fori_loop(0, wide // rows, body, 0)
    if room > wide:
        gap = jnp.zeros((room - wide, out.shape[1]), LOW)
        out[wide:room, :] = gap
        out[room + wide:, :] = gap


def backward(kept, got, up_out, up_tangent, cotangent, cot_tangent):
    return pl.pallas_call(
        backward_kernel,
        out_shape=jax.ShapeDtypeStruct(kept.shape, LOW),
        in_specs=[VMEM] * 6,
        out_specs=VMEM,
        compiler_params=pltpu.CompilerParams(vmem_limit_bytes=24 * 2**20),
        cost_estimate=pl.CostEstimate(
            flops=20 * kept.size, bytes_accessed=14 * kept.size, transcendentals=kept.size // 2
        ),
    )(kept, got, up_out, up_tangent, cotangent, cot_tangent)


def gate_kernel(count, *refs):
    pieces, rows, kept, away = refs[:count], refs[count:-2], refs[-2], refs[-1]
    mine = kept.shape[1]
    tile = next(n for n in (256, 128, 64) if kept.shape[0] % n == 0)

    def body(i, carry):
        at = pl.ds(pl.multiple_of(i * tile, tile), tile)
        total = None
        for piece, row in zip(pieces, rows):
            part = dot(piece[:, at], row[...], ((0,), (0,)))
            total = part if total is None else total + part
        kept[at, :] = total[:, :mine]
        away[at, :] = total[:, mine:]
        return carry

    lax.fori_loop(0, kept.shape[0] // tile, body, 0)


def gate_products(pieces, rows):
    columns, mine = pieces[0].shape[1], rows[0].shape[1] // 2
    depth = sum(p.shape[0] for p in pieces)
    return pl.pallas_call(
        functools.partial(gate_kernel, len(pieces)),
        out_shape=(jax.ShapeDtypeStruct((columns, mine), F32),) * 2,
        in_specs=[VMEM] * (2 * len(pieces)),
        out_specs=(VMEM, VMEM),
        compiler_params=pltpu.CompilerParams(vmem_limit_bytes=24 * 2**20),
        cost_estimate=pl.CostEstimate(
            flops=4 * depth * columns * mine,
            bytes_accessed=2 * depth * (columns + 2 * mine) + 8 * columns * mine,
            transcendentals=0,
        ),
    )(*pieces, *rows)


def place_kernel(spots, order, *refs):
    pieces, out, sems = refs[:len(spots)], refs[-2], refs[-1]
    copies = [
        pltpu.make_async_copy(
            piece, out.at[order[j], pl.ds(row, piece.shape[0])], sems.at[i]
        )
        for i, (piece, (j, row)) in enumerate(zip(pieces, spots))
    ]
    for copy in copies:
        copy.start()
    for copy in copies:
        copy.wait()


def place(order, spots, pieces, rows, into=None):
    columns = pieces[0].shape[1]
    extra = [] if into is None else [into]
    return pl.pallas_call(
        functools.partial(place_kernel, spots),
        out_shape=jax.ShapeDtypeStruct((8, rows, columns), LOW),
        in_specs=[SMEM] + [ANY] * (len(pieces) + len(extra)),
        out_specs=ANY,
        input_output_aliases={1 + len(pieces): 0} if extra else {},
        scratch_shapes=[pltpu.SemaphoreType.DMA((len(pieces),))],
        compiler_params=pltpu.CompilerParams(vmem_limit_bytes=24 * 2**20),
        cost_estimate=pl.CostEstimate(
            flops=0, bytes_accessed=4 * sum(p.size for p in pieces), transcendentals=0
        ),
    )(order, *pieces, *extra)


def add_rows(total, part, start):
    rows = part.shape[0]
    pieces = [total[start:start + rows] + part.astype(F32)]
    if start:
        pieces.insert(0, total[:start])
    if start + rows < total.shape[0]:
        pieces.append(total[start + rows:])
    return jnp.concatenate(pieces, axis=0)


def on_device(tokens, up_out, up_tangent, cotangent, cot_tangent, gate_weight, gate_direction):
    xl, y, c, z, xh = (lax.axis_index(name) for name in AXES)
    depth, wide = gate_weight.shape
    mine = tokens.shape[0]
    half = depth // 2
    same = c == xh
    sign = 1 - 2 * c

    room = -(-wide // 128) * 128
    gap = ((0, 0), (0, room - wide))
    own = jnp.concatenate([jnp.pad(gate_weight, gap), jnp.pad(gate_direction, gap)], axis=1)

    own, turned = after(own, tokens.T)
    near = lax.ppermute(turned, ("c", "xh"), [(2, 0), (1, 3), (0, 1), (3, 2)])
    cross = lax.ppermute(turned, ("c", "xh"), [(2, 1), (1, 2)])
    block = jnp.concatenate([jnp.where(same, turned, near), jnp.where(same, near, cross)], axis=1)

    one = step(own, "y", 1)
    over = swap(own, "xl")
    later, block = after(own, block)
    two = step(later, "y", -1)
    a1, b1 = step(block, "z", 1), step(block, "z", -1)
    one, a1, b1 = after(one, a1, b1)
    a2, b2 = step(a1, "z", 1), step(b1, "z", -1)
    far_one = step(one[:half], "y", 1)
    a3, b3 = step(a2, "z", 1), step(b2, "z", -1)
    far_two = step(two[half:], "y", -1)
    a4, b4 = step(a3[:half], "z", 1), step(b3[half:], "z", -1)
    over, far_one = after(over, far_one)
    over_far_one = swap(far_one, "xl")
    over_one = step(over, "y", 1)
    over, far_two = after(over, far_two)
    over_far_two = swap(far_two, "xl")
    over_two = step(over, "y", -1)
    opposite = jnp.concatenate([a4, b4], axis=0)
    token_blocks = jnp.stack([block, b1, b2, b3, opposite, a3, a2, a1])

    index = jnp.stack([
        (sign * (jnp.bitwise_xor(xl, j // 4) * 4 + (y + sign * j + 8) % 4 - z) + 16) % 8
        for j in range(8)
    ])
    rows_of = [
        lax.dynamic_index_in_dim(token_blocks, index[j], 0, keepdims=False) for j in range(8)
    ]
    early = [(own, 0, 0), (over, 4, 0), (one, 3, 0), (two, 1, 0), (far_one, 2, 0), (far_two, 2, half)]
    late = [(over_far_one, 6, 0), (over_one, 7, 0), (over_far_two, 6, half), (over_two, 5, 0)]
    spots, pieces = [g[1:] for g in early], [g[0] for g in early]
    along = place(index, spots, pieces, depth)
    kept, away = gate_products(
        pieces, [rows_of[j][row:row + piece.shape[0]] for piece, j, row in early]
    )
    along, kept = after(along, kept)
    for piece, j, row in late:
        rows = rows_of[j][row:row + piece.shape[0]]
        kept, away, piece, rows = after(kept, away, piece, rows)
        away = away + dot(piece, rows[:, mine:], ((0,), (0,)))
        if j != 5:
            kept = kept + dot(piece, rows[:, :mine], ((0,), (0,)))
    got = swap(away.astype(LOW), "c")
    kept = kept + dot(piece, rows[:, :mine], ((0,), (0,)))
    spots, pieces = [g[1:] for g in late], [g[0] for g in late]
    along = place(index, spots, pieces, depth, along)
    got, along = after(got, along)

    mixed = backward(kept, got, up_out.T, up_tangent.T, cotangent.T, cot_tangent.T)
    other = swap(mixed, "c")

    everyone = jnp.concatenate([mixed, other], axis=1)

    def tangent(offset):
        return dot(along[offset % 8], everyone, ((1,), (0,)))

    opposite, late = after(tangent(4).astype(LOW), everyone)
    chain_a = step(opposite, "z", 1)
    chain_b = step(dot(along[5], late, ((1,), (0,))).astype(LOW), "z", -1)
    sum_a = (tangent(3) + chain_a.astype(F32)).astype(LOW)
    back_dot, sum_a = after(everyone[:wide], sum_a)
    chain_a = step(sum_a, "z", 1)

    def curv(other, offset):
        return dot(rows_of[other * 4 + offset], back_dot, ((1,), (1,)))

    got_x = swap(curv(1, 2).astype(LOW), "xl")
    got_one = step(curv(1, 1).astype(LOW), "y", 1)
    got_two = step(curv(1, 3).astype(LOW), "y", -1)
    second_a, second_b, sum_b = after(tangent(2), tangent(-2), chain_b)
    chain_b = step((second_b + sum_b.astype(F32)).astype(LOW), "z", -1)
    first_a, first_b, at_home, sum_a = after(tangent(1), tangent(-1), tangent(0), chain_a)
    chain_a = step((second_a + sum_a.astype(F32)).astype(LOW), "z", 1)
    far_sum = (curv(0, 2) + got_x.astype(F32)).astype(LOW)
    far_one = step(far_sum[:half], "y", 1)
    far_two = step(far_sum[half:], "y", -1)
    chain_b = step((first_b + chain_b.astype(F32)).astype(LOW), "z", -1)
    chain_a = step((first_a + chain_a.astype(F32)).astype(LOW), "z", 1)
    over_sum = (curv(1, 0) + got_one.astype(F32) + got_two.astype(F32)).astype(LOW)
    last_x = swap(over_sum, "xl")
    last_one = step(add_rows(curv(0, 1), far_one, 0).astype(LOW), "y", 1)
    last_two = step(add_rows(curv(0, 3), far_two, half).astype(LOW), "y", -1)
    total = at_home + chain_a.astype(F32) + chain_b.astype(F32)
    of_own, of_other = total[:, :mine], total[:, mine:]
    sent = jnp.where(same, of_other, of_own).astype(LOW)
    near = lax.ppermute(sent, ("c", "xh"), [(1, 0), (2, 3), (0, 2), (3, 1)])
    cross = lax.ppermute(of_other.astype(LOW), ("c", "xh"), [(1, 2), (2, 1)])
    rest = jnp.where(same, of_own, cross.astype(F32))
    input_tangent = (rest + near.astype(F32)).astype(LOW).T

    curvature = (
        curv(0, 0) + last_x.astype(F32) + last_one.astype(F32) + last_two.astype(F32)
    ).astype(LOW)
    return (curvature, input_tangent)


def solution(mesh):
    fine = Mesh(mesh.devices.reshape([SIZES[name] for name in AXES]), AXES)
    spec = P(("xl", "y", "c"), ("z", "xh"))
    return jax.shard_map(
        on_device, mesh=fine, in_specs=(spec,) * 7, out_specs=(spec, spec), check_vma=False
    )
```
